32 devices in a mesh: grp: 4 (over y, x), tok: 2 (over core), head: 4 (over z).
Axes of the slice: x: 2, y: 2, z: 4, core: 2. Of those that a mesh axis runs over, the one named last changes fastest.
Arguments:
- tokens: bfloat16 [4, 256, 1024], P('grp', 'tok'), may hold values from -6 to 6
- lengths: int32 [4, 8], P('grp'), may hold values from 1 to 192, 256 in all within a row
- block_position: int32 [4, 32], P('grp'), may hold values from 0 to 31, each once within a row
- prefix_pool: bfloat16 [4, 32, 16, 2, 1024], P('grp', ('tok', 'head'))
- cross_cache: bfloat16 [4, 256, 2, 1024], P('grp', None, None, 'head')
- w_query: bfloat16 [1024, 1024], P(None, 'head'), may hold values from -0.5 to 0.5
- w_keyvalue: bfloat16 [1024, 2, 1024], P(None, None, 'head'), may hold values from -0.1875 to 0.1875
- w_out: bfloat16 [1024, 1024], P('head'), may hold values from -0.1875 to 0.1875
- w_cross_query: bfloat16 [1024, 1024], P(None, 'head'), may hold values from -0.5 to 0.5
- w_cross_out: bfloat16 [1024, 1024], P('head'), may hold values from -0.1875 to 0.1875
- w_up: bfloat16 [1024, 8192], P(None, 'head'), may hold values from -0.1875 to 0.1875
- w_down: bfloat16 [8192, 1024], P('head'), may hold values from -0.0625 to 0.0625
Outputs:
- layer_out: bfloat16 [4, 256, 1024], P('grp', ('tok', 'head'))
The draws below stay inside these ranges and needn't reach their ends.
Inputs may be any that keep to these rules, and one draw needn't show every extreme that they name: Each group's 8 lengths sum to 256; the longest is exactly 192. `block_position`: each group's row is a permutation of 0 to 31.
All inputs are finite; a program needn't handle non-finite values.
Results may differ from the reference program's by a relative error of at most 0.034.
The reference program's roundings to bfloat16 on the way count: a program that leaves them out, or rounds other values in their place, can miss the bound.
Values may be sent and summed in bfloat16 or wider, within the bound.
No kernel may reach another device: no remote copies, remote signals or barrier semaphores. Data moves between devices by JAX's collectives and lax.ppermute only.
A program may use at most 128 MiB of HBM per device.

```python
import math
import jax
import jax.numpy as jnp
import numpy as np
from jax import lax

D = 1024
HEADS = 16
HEAD_DIM = 64
FF = 8192
TOK_DEV = 128
E = 256
BLK = 16
SINK = 4
REQS = 8
GROUPS = 4
SUFFIX = 256
NBLOCKS = 32
PREFIX = 512
WINDOW = 1024


def boosted_cache(key, lead_shape, value_scale):
    normal_draw = jax.random.truncated_normal(jax.random.fold_in(key, 11), -6.0, 6.0, lead_shape + (2, D), jnp.float32)
    half_scale = jnp.where(jnp.arange(2)[:, None] == 0, 1.0, value_scale).astype(jnp.float32)
    normal_draw = normal_draw * half_scale
    return normal_draw


def draw_prefix_pool(key, part):
    return boosted_cache(key, (GROUPS, NBLOCKS, BLK), 3.0).astype(jnp.bfloat16)


def draw_cross_cache(key, part):
    return boosted_cache(key, (GROUPS, E), 1.0).astype(jnp.bfloat16)


def shard_levels(rng, extent, split, low, top_value):
    def one(position, parts):
        steps = jax.random.uniform(jax.random.fold_in(jax.random.fold_in(rng, 6), position), (parts,), jnp.float32, low / len(split), top_value / len(split))
        return jnp.repeat(jnp.exp(steps), extent[position] // parts).reshape((-1,) + (1,) * (len(extent) - position - 1))

    level = one(*split[0])
    for cut in split[1:]:
        level = level * one(*cut)
    return level


def profile(count, total, bound, lean):
    portions = [(1 << 20) // math.isqrt(rank ** lean) + 1 for rank in range(2, count + 1)]
    spare, given = total - bound - (count - 1), [1] * (count - 1)
    while spare > 0:
        free = [i for i in range(count - 1) if given[i] < bound]
        mass, remaining = sum([portions[i] for i in free]), spare
        for i in free:
            extra = min(bound - given[i], max(1, remaining * portions[i] // mass), spare)
            given[i] = given[i] + extra
            spare = spare - extra
    return np.array([bound] + given)


def ragged_sizes(stream_key, number_of, total, reach, lean):
    if number_of == 2:
        one = jax.random.randint(stream_key, (), max(1, total - reach), min(reach, total - 1) + 1)
        return jnp.stack([one, total - one])
    sizes = jnp.asarray(profile(number_of, total, reach, lean), jnp.int32)
    pairs = (number_of - 1) // 2
    giver, receiver = sizes[1:1 + 2 * pairs:2], sizes[2:2 + 2 * pairs:2]
    room = jnp.minimum(giver - 1, reach - receiver)
    shifted = jax.random.randint(jax.random.fold_in(stream_key, 1), (pairs,), 0, 1 << 20) % (room + 1)
    sizes = sizes.at[1:1 + 2 * pairs:2].set(giver - shifted).at[2:2 + 2 * pairs:2].set(receiver + shifted)
    return sizes[jax.random.permutation(jax.random.fold_in(stream_key, 2), number_of)]


def gaussian(rng, dims, width, bound, split=(), kind=jnp.bfloat16):
    drawn = width * jax.random.normal(rng, dims, jnp.float32)
    if split:
        drawn = drawn * shard_levels(rng, dims, split, -0.22, 0.18)
    return jnp.clip(drawn, -bound, bound).astype(kind)


def setup_inputs(seed: int = 0) -> dict:
    splits = jax.random.split(jax.random.key(seed), 13)
    return {
        "tokens": gaussian(splits[0], (GROUPS, SUFFIX, D), 1.0, 6.0, ((0, 4), (1, 2))),
        "lengths": jax.vmap(lambda own: ragged_sizes(own, REQS, SUFFIX, SUFFIX * 3 // 4, 2))(jax.random.split(splits[1], GROUPS)).reshape((GROUPS, REQS)).astype(jnp.int32),
        "block_position": jax.vmap(lambda own: jax.random.permutation(own, NBLOCKS))(jax.random.split(splits[2], GROUPS)).reshape((GROUPS, NBLOCKS)).astype(jnp.int32),
        "prefix_pool": draw_prefix_pool(jax.random.fold_in(splits[12], 71), 0),
        "cross_cache": draw_cross_cache(jax.random.fold_in(splits[12], 71), 0),
        "w_query": gaussian(splits[5], (D, D), (D // 8) ** -0.5, 0.5, ((1, 4),)),
        "w_keyvalue": gaussian(splits[6], (D, 2, D), D ** -0.5, 0.1875, ((2, 4),)),
        "w_out": gaussian(splits[7], (D, D), D ** -0.5, 0.1875, ((0, 4),)),
        "w_cross_query": gaussian(splits[8], (D, D), (D // 8) ** -0.5, 0.5, ((1, 4),)),
        "w_cross_out": gaussian(splits[9], (D, D), D ** -0.5, 0.1875, ((0, 4),)),
        "w_up": gaussian(splits[10], (D, FF), D ** -0.5, 0.1875, ((1, 4),)),
        "w_down": gaussian(splits[11], (FF, D), FF ** -0.5, 0.0625, ((0, 4),)),
    }


eps = 1e-05
masked = -1e+30

def layer_norm(values):
    center = values - lax.optimization_barrier(jnp.mean(values, axis=-1, keepdims=True))
    spread = lax.optimization_barrier(jnp.mean(center * center, axis=-1, keepdims=True))
    return center * lax.rsqrt(spread + eps)

def request_info(token_ids, lengths_row):
    request_ends = jnp.cumsum(lengths_row, dtype=jnp.int32)
    before = request_ends[None, :] <= token_ids[:, None]
    request = lax.optimization_barrier(jnp.sum(before.astype(jnp.int32), axis=1, dtype=jnp.int32))
    first_token = lax.optimization_barrier(jnp.sum(jnp.where(before, lengths_row[None, :], 0), axis=1, dtype=jnp.int32))
    return (request, token_ids - first_token)

def softmax_heads(queries, key_heads, value_heads, allowed, score_scale):
    scores = jnp.einsum('qhd,khd->hqk', queries.astype(jnp.float32), key_heads.astype(jnp.float32)) * score_scale
    scores = jnp.where(allowed[None], scores, masked)
    row_max = lax.optimization_barrier(jnp.max(scores, axis=-1))
    weights = jnp.where(allowed[None], jnp.exp(scores - row_max[..., None]), 0.0)
    row_sum = lax.optimization_barrier(jnp.sum(weights, axis=-1))
    summed = jnp.einsum('hqk,khd->hqd', weights.astype(jnp.bfloat16).astype(jnp.float32), value_heads.astype(jnp.float32))
    result = summed / row_sum[..., None]
    return jnp.transpose(result, (1, 0, 2)).reshape(queries.shape[0], -1).astype(jnp.bfloat16)

def reference(tokens, lengths, block_position, prefix_pool, cross_cache, w_query, w_keyvalue, w_out, w_cross_query, w_cross_out, w_up, w_down):
    score_scale = HEAD_DIM ** (-0.5)
    outputs = []
    for group_index in range(GROUPS):
        residual = tokens[group_index].astype(jnp.float32)
        normed = layer_norm(residual).astype(jnp.bfloat16)
        queries = jnp.dot(normed, w_query, preferred_element_type=jnp.float32).astype(jnp.bfloat16)
        keyvalue = jnp.dot(normed, w_keyvalue.reshape(D, 2 * D), preferred_element_type=jnp.float32).astype(jnp.bfloat16).reshape(SUFFIX, 2, D)
        lengths_row = lengths[group_index]
        all_ids = jnp.arange(SUFFIX, dtype=jnp.int32)
        request, offset = request_info(all_ids, lengths_row)
        padded = jnp.concatenate([jnp.zeros((WINDOW, 2, D), jnp.bfloat16), keyvalue], axis=0)
        block_table = block_position[group_index]
        places = (block_table[:, None] * BLK + jnp.arange(BLK, dtype=jnp.int32)[None, :]).reshape(-1)
        pool = prefix_pool[group_index].reshape(PREFIX, 2, D)

        def one_block(block_index):
            first_row = (block_index * TOK_DEV).astype(jnp.int32)
            own_ids = first_row + jnp.arange(TOK_DEV, dtype=jnp.int32)
            own_request = lax.dynamic_slice_in_dim(request, first_row, TOK_DEV, 0)
            own_offset = lax.dynamic_slice_in_dim(offset, first_row, TOK_DEV, 0)
            block_queries = lax.dynamic_slice_in_dim(queries, first_row, TOK_DEV, 0).reshape(TOK_DEV, HEADS, HEAD_DIM)
            near_keys = lax.dynamic_slice_in_dim(padded, first_row, WINDOW + TOK_DEV, 0)
            near_ids = first_row - WINDOW + jnp.arange(WINDOW + TOK_DEV, dtype=jnp.int32)
            near_request = request_info(near_ids, lengths_row)[0]
            near_allowed = (near_ids[None, :] >= 0) & (near_request[None, :] == own_request[:, None]) & (near_ids[None, :] <= own_ids[:, None]) & (own_ids[:, None] - near_ids[None, :] < WINDOW)
            prefix_allowed = (places[None, :] < SINK) | (places[None, :] > PREFIX + own_offset[:, None] - WINDOW)
            all_keys = jnp.concatenate([near_keys, pool], axis=0)
            allowed = jnp.concatenate([near_allowed, prefix_allowed], axis=1)
            key_heads = all_keys[:, 0].reshape(-1, HEADS, HEAD_DIM)
            value_heads = all_keys[:, 1].reshape(-1, HEADS, HEAD_DIM)
            return softmax_heads(block_queries, key_heads, value_heads, allowed, score_scale)
        attended = lax.map(one_block, jnp.arange(SUFFIX // TOK_DEV, dtype=jnp.int32)).reshape(SUFFIX, D)
        after_self = residual + jnp.dot(attended, w_out, preferred_element_type=jnp.float32)
        cross_query = jnp.dot(layer_norm(after_self).astype(jnp.bfloat16), w_cross_query, preferred_element_type=jnp.float32).astype(jnp.bfloat16)
        cross_keys = cross_cache[group_index][:, 0].reshape(E, HEADS, HEAD_DIM)
        cross_values = cross_cache[group_index][:, 1].reshape(E, HEADS, HEAD_DIM)
        cross_allowed = jnp.ones((SUFFIX, E), dtype=bool)
        cross_out = softmax_heads(cross_query.reshape(SUFFIX, HEADS, HEAD_DIM), cross_keys, cross_values, cross_allowed, score_scale)
        after_cross = after_self + jnp.dot(cross_out, w_cross_out, preferred_element_type=jnp.float32)
        hidden = jax.nn.relu(jnp.dot(layer_norm(after_cross).astype(jnp.bfloat16), w_up, preferred_element_type=jnp.float32)).astype(jnp.bfloat16)
        result = after_cross + jnp.dot(hidden, w_down, preferred_element_type=jnp.float32)
        outputs.append(result.astype(jnp.bfloat16))
    return jnp.stack(outputs, axis=0)
```

```python
import jax
import jax.numpy as jnp
from jax import lax
from jax.sharding import PartitionSpec as P

HEAD_DIM = 64
SPAN = 8
SINK = 4
WINDOW = 1024


eps = 1e-05
masked = -1e30


def from_behind(array, axis, by):
    count = lax.axis_size(axis)
    pairs = [(i, i + by) for i in range(count) if 0 <= i + by < count]
    return lax.ppermute(array, axis, pairs)


def swap(array, axis, by):
    count = lax.axis_size(axis)
    return lax.ppermute(array, axis, [(i, i ^ by) for i in range(count)])


def gather_heads(array):
    count = lax.axis_size("head")
    return [array] + [swap(array, "head", by) for by in range(1, count)]


def scatter_heads(pieces):
    return pieces[:1] + [swap(piece, "head", by) for by, piece in enumerate(pieces) if by]


def layer_norm(values):
    center = values - jnp.mean(values, axis=-1, keepdims=True)
    spread = jnp.mean(center * center, axis=-1, keepdims=True)
    return center * lax.rsqrt(spread + eps)


def request_info(token_ids, lengths_row):
    request_ends = jnp.cumsum(lengths_row, dtype=jnp.int32)
    before = request_ends[None, :] <= token_ids[:, None]
    request = jnp.sum(before.astype(jnp.int32), axis=1, dtype=jnp.int32)
    first_token = jnp.sum(jnp.where(before, lengths_row[None, :], 0), axis=1, dtype=jnp.int32)
    return (request, token_ids - first_token)


def attend_block(queries, key_heads, value_heads, allowed, score_scale):
    scores = (
        jnp.einsum("qhd,khd->hqk", queries, key_heads, preferred_element_type=jnp.float32)
        * score_scale
    )
    scores = jnp.where(allowed[None], scores, masked)
    row_max = jnp.max(scores, axis=-1)
    weights = jnp.where(allowed[None], jnp.exp(scores - row_max[..., None]), 0.0)
    row_sum = jnp.sum(weights, axis=-1)
    summed = jnp.einsum(
        "hqk,khd->hqd",
        weights.astype(jnp.bfloat16),
        value_heads,
        preferred_element_type=jnp.float32,
    )
    return (row_max, row_sum, summed)


def combine(earlier, later):
    row_max = jnp.maximum(earlier[0], later[0])
    left_scale = jnp.exp(earlier[0] - row_max)
    right_scale = jnp.exp(later[0] - row_max)
    row_sum = earlier[1] * left_scale + later[1] * right_scale
    summed = earlier[2] * left_scale[..., None] + later[2] * right_scale[..., None]
    return (row_max, row_sum, summed)


def finish(partial_value, row_count, group_width):
    result = partial_value[2] / partial_value[1][..., None]
    return jnp.transpose(result, (1, 0, 2)).reshape(row_count, group_width).astype(jnp.bfloat16)


def on_device(
    tokens,
    lengths,
    block_position,
    prefix_pool,
    cross_cache,
    w_query,
    w_keyvalue,
    w_out,
    w_cross_query,
    w_cross_out,
    w_up,
    w_down,
):
    row_total = tokens.shape[1]
    model_width = tokens.shape[2]
    group_width = w_query.shape[1]
    heads_here = group_width // HEAD_DIM
    score_scale = HEAD_DIM ** (-0.5)
    tok_index = lax.axis_index("tok")
    head_index = lax.axis_index("head")
    head_count = lax.axis_size("head")
    tok_count = lax.axis_size("tok")
    share_rows = row_total // head_count
    lengths_row = lengths[0]
    residual = tokens[0].astype(jnp.float32)
    normed = layer_norm(residual).astype(jnp.bfloat16)
    queries = (
        jnp.dot(normed, w_query, preferred_element_type=jnp.float32)
        .astype(jnp.bfloat16)
        .reshape(row_total, heads_here, HEAD_DIM)
    )
    keyvalue = (
        jnp.dot(
            normed,
            w_keyvalue.reshape(model_width, 2 * group_width),
            preferred_element_type=jnp.float32,
        )
        .astype(jnp.bfloat16)
        .reshape(row_total, 2, group_width)
    )
    own_ids = tok_index * row_total + jnp.arange(row_total, dtype=jnp.int32)
    own_request, own_offset = request_info(own_ids, lengths_row)
    key_blocks = [keyvalue]
    key_ids = [own_ids]
    for distance in range(1, min(SPAN, tok_count - 1) + 1):
        key_blocks.append(from_behind(keyvalue, "tok", distance))
        key_ids.append((tok_index - distance) * row_total + jnp.arange(row_total, dtype=jnp.int32))
    near_keys = jnp.concatenate(key_blocks, axis=0)
    near_ids = jnp.concatenate(key_ids, axis=0)
    near_request = request_info(near_ids, lengths_row)[0]
    near_allowed = (
        (near_ids[None, :] >= 0)
        & (near_request[None, :] == own_request[:, None])
        & (near_ids[None, :] <= own_ids[:, None])
        & (own_ids[:, None] - near_ids[None, :] < WINDOW)
    )
    suffix_part = attend_block(
        queries,
        near_keys[:, 0].reshape(-1, heads_here, HEAD_DIM),
        near_keys[:, 1].reshape(-1, heads_here, HEAD_DIM),
        near_allowed,
        score_scale,
    )
    blocks_total = block_position.shape[1]
    block_len = prefix_pool.shape[2]
    prefix_len = blocks_total * block_len
    block_table = block_position[0]
    start_carry = (
        jnp.full((heads_here, row_total), masked, jnp.float32),
        jnp.zeros((heads_here, row_total), jnp.float32),
        jnp.zeros((heads_here, row_total, HEAD_DIM), jnp.float32),
    )
    shard_blocks = prefix_pool.shape[1]
    own_pool = prefix_pool[0]
    pieces = scatter_heads(
        [
            lax.dynamic_slice_in_dim(own_pool, (head_index ^ by) * group_width, group_width, 3)
            for by in range(head_count)
        ]
    )
    own_columns = jnp.concatenate(pieces, axis=0)
    columns = jnp.concatenate(
        [own_columns] + [swap(own_columns, "tok", by) for by in range(1, tok_count)], axis=0
    )
    slot_blocks = columns.shape[0]
    physical = jnp.concatenate(
        [
            ((tok_index ^ far) * head_count + (head_index ^ by)) * shard_blocks
            + jnp.arange(shard_blocks, dtype=jnp.int32)
            for far in range(tok_count)
            for by in range(head_count)
        ]
    )
    logical = jnp.sum(
        jnp.where(
            physical[:, None] == jnp.arange(blocks_total, dtype=jnp.int32)[None, :],
            block_table[None, :],
            0,
        ),
        axis=1,
        dtype=jnp.int32,
    )
    places = (
        logical[:, None] * block_len + jnp.arange(block_len, dtype=jnp.int32)[None, :]
    ).reshape(-1)
    flat_slots = columns.reshape(slot_blocks * block_len, 2, heads_here, HEAD_DIM)
    allowed = (places[None, :] < SINK) | (
        places[None, :] > prefix_len + own_offset[:, None] - WINDOW
    )
    prefix_part = combine(
        start_carry, attend_block(queries, flat_slots[:, 0], flat_slots[:, 1], allowed, score_scale)
    )
    attended = finish(combine(suffix_part, prefix_part), row_total, group_width)
    cross_keys = cross_cache[0][:, 0].reshape(-1, heads_here, HEAD_DIM)
    cross_values = cross_cache[0][:, 1].reshape(-1, heads_here, HEAD_DIM)

    def row_share(array, by):
        return lax.dynamic_slice_in_dim(array, (head_index ^ by) * share_rows, share_rows, 0)

    def heads_total(partial_term):
        partial_term = partial_term.astype(jnp.bfloat16)
        terms = scatter_heads([row_share(partial_term, by) for by in range(head_count)])
        return sum(term.astype(jnp.float32) for term in terms)

    after_self = row_share(residual, 0) + heads_total(
        jnp.dot(attended, w_out, preferred_element_type=jnp.float32)
    )
    normed_cross = jnp.concatenate(gather_heads(layer_norm(after_self).astype(jnp.bfloat16)), 0)
    cross_query = jnp.dot(
        normed_cross,
        w_cross_query,
        preferred_element_type=jnp.float32,
    ).astype(jnp.bfloat16)
    query_rows = cross_query.shape[0]
    allowed = jnp.ones((query_rows, cross_keys.shape[0]), dtype=bool)
    partial_value = attend_block(
        cross_query.reshape(query_rows, heads_here, HEAD_DIM),
        cross_keys,
        cross_values,
        allowed,
        score_scale,
    )
    cross_out = finish(partial_value, query_rows, group_width)
    cross_partial = jnp.dot(cross_out, w_cross_out, preferred_element_type=jnp.float32).astype(
        jnp.bfloat16
    )
    cross_terms = scatter_heads(
        [cross_partial[by * share_rows : (by + 1) * share_rows] for by in range(head_count)]
    )
    after_cross = after_self + sum(term.astype(jnp.float32) for term in cross_terms)
    normed_hidden = jnp.concatenate(gather_heads(layer_norm(after_cross).astype(jnp.bfloat16)), 0)
    hidden = jax.nn.relu(
        jnp.dot(normed_hidden, w_up, preferred_element_type=jnp.float32)
    ).astype(jnp.bfloat16)
    down = jnp.dot(hidden, w_down, preferred_element_type=jnp.float32).astype(jnp.bfloat16)
    down_terms = scatter_heads(
        [down[by * share_rows : (by + 1) * share_rows] for by in range(head_count)]
    )
    result = after_cross + sum(term.astype(jnp.float32) for term in down_terms)
    return result.astype(jnp.bfloat16)[None]


def solution(mesh):
    return jax.shard_map(
        on_device,
        mesh=mesh,
        in_specs=(
            P("grp", "tok", None),
            P("grp", None),
            P("grp", None),
            P("grp", ("tok", "head"), None, None, None),
            P("grp", None, None, "head"),
            P(None, "head"),
            P(None, None, "head"),
            P("head", None),
            P(None, "head"),
            P("head", None),
            P(None, "head"),
            P("head", None),
        ),
        out_specs=P("grp", ("tok", "head"), None),
        check_vma=False,
    )
```

```python
import functools

import jax
import jax.numpy as jnp
from jax import lax
from jax.experimental import pallas as pl
from jax.experimental.pallas import tpu as pltpu
from jax.sharding import PartitionSpec as P

HEAD_DIM = 64
SPAN = 8
SINK = 4
WINDOW = 1024
SCALE = HEAD_DIM ** (-0.5)
EPS = 1e-05
VMEM_BYTES = 48 << 20
WIDE_SCORES = 8 << 20

bf16 = jnp.bfloat16
f32 = jnp.float32
i32 = jnp.int32


def swap(array, axis, by):
    count = lax.axis_size(axis)
    return lax.ppermute(array, axis, [(i, i ^ by) for i in range(count)])


def from_behind(array, axis, by):
    count = lax.axis_size(axis)
    return lax.ppermute(array, axis, [(i, (i + by) % count) for i in range(count)])


def gather_heads(array):
    return [array] + [swap(array, "head", by) for by in range(1, lax.axis_size("head"))]


def scatter_heads(pieces):
    return [pieces[0]] + [swap(piece, "head", by) for by, piece in enumerate(pieces) if by]


def kernel_call(body, outs, flops, *args):
    smem = {jnp.dtype(i32)}
    return pl.pallas_call(
        body,
        out_shape=outs,
        in_specs=[
            pl.BlockSpec(memory_space=pltpu.SMEM if a.dtype in smem else pltpu.VMEM) for a in args
        ],
        compiler_params=pltpu.CompilerParams(vmem_limit_bytes=VMEM_BYTES),
        cost_estimate=pl.CostEstimate(
            flops=flops, bytes_accessed=sum(a.nbytes for a in args), transcendentals=0
        ),
    )(*args)


def layer_norm(values):
    center = values - jnp.mean(values, axis=-1, keepdims=True)
    spread = jnp.mean(center * center, axis=-1, keepdims=True)
    return center * lax.rsqrt(spread + EPS)


def dot(left, right):
    return jnp.dot(left, right, preferred_element_type=f32)


def split_pair(pairs):
    rows, _, width = pairs.shape
    flat = pairs.astype(f32).reshape(rows, 2 * width).astype(bf16)
    return flat[:, :width], flat[:, width:]


def head_lanes(shape):
    return lax.broadcasted_iota(i32, shape, len(shape) - 1) // HEAD_DIM


def attend_heads(queries, keys, values, allowed, heads):
    rows, width = queries.shape
    lanes = head_lanes((rows, width))
    stacked = jnp.concatenate(
        [jnp.where(lanes == h, queries, jnp.zeros_like(queries)) for h in heads], axis=0
    )
    scores = lax.dot_general(
        stacked, keys, (((1,), (1,)), ((), ())), preferred_element_type=f32
    ).reshape(len(heads), rows, keys.shape[0])
    scores = scores * SCALE
    if allowed is not None:
        scores = jnp.where(allowed[None], scores, -jnp.inf)
    row_max = jnp.max(scores, axis=-1, keepdims=True)
    weights = jnp.exp(scores - row_max)
    row_sum = jnp.sum(weights, axis=-1, keepdims=True)
    summed = dot(weights.astype(bf16).reshape(len(heads) * rows, -1), values)
    summed = summed.reshape(len(heads), rows, width) / row_sum
    result = jnp.zeros((rows, width), f32)
    for i, h in enumerate(heads):
        result = jnp.where(lanes == h, summed[i], result)
    return result


def attend(queries, keys, values, allowed):
    rows, width = queries.shape
    heads = list(range(width // HEAD_DIM))
    if len(heads) * rows * keys.shape[0] * 4 <= WIDE_SCORES:
        return attend_heads(queries, keys, values, allowed, heads).astype(bf16)
    result = attend_heads(queries, keys, values, allowed, heads[:1])
    for h in heads[1:]:
        result = result + attend_heads(queries, keys, values, allowed, [h])
    return result.astype(bf16)


def project_body(tokens, w_query, w_keyvalue, queries, keyvalue):
    normed = layer_norm(tokens[0].astype(f32)).astype(bf16)
    queries[...] = dot(normed, w_query[...]).astype(bf16)
    w_key, w_value = split_pair(w_keyvalue[...])
    width = w_key.shape[1]
    keyvalue[:, :width] = dot(normed, w_key).astype(bf16)
    keyvalue[:, width:] = dot(normed, w_value).astype(bf16)


def request_info(token_ids, lengths):
    request = jnp.zeros_like(token_ids)
    first_token = jnp.zeros_like(token_ids)
    end = jnp.int32(0)
    for i in range(lengths.shape[1]):
        end = end + lengths[0, i]
        before = end <= token_ids
        request = request + before.astype(i32)
        first_token = jnp.where(before, first_token + lengths[0, i], first_token)
    return request, token_ids - first_token


def self_body(near, head_count, tok_count, place, lengths, table, queries, w_out, *refs):
    tok_index, head_index = place[0], place[1]
    near_refs, refs = refs[:near], refs[near:]
    slot_refs, outs = refs[:-head_count], refs[-head_count:]
    rows, width = queries.shape
    own_ids = tok_index * rows + lax.broadcasted_iota(i32, (rows, 1), 0)
    own_request, own_offset = request_info(own_ids, lengths)
    keys, values, allowed = [], [], []
    for distance, ref in enumerate(near_refs):
        keys.append(ref[:, :width])
        values.append(ref[:, width:])
        ids = (tok_index - distance) * rows + lax.broadcasted_iota(i32, (1, rows), 1)
        allowed.append(
            (ids >= 0)
            & (request_info(ids, lengths)[0] == own_request)
            & (ids <= own_ids)
            & (own_ids - ids < WINDOW)
        )
    block_len = slot_refs[0].shape[1]
    shard_blocks = slot_refs[0].shape[0]
    prefix_len = table.shape[1] * block_len
    piece_of = 0
    for ref in slot_refs:
        count = ref.shape[0] * block_len
        key, value = split_pair(ref[...].reshape(count, 2, width))
        keys.append(key)
        values.append(value)
        slot = lax.broadcasted_iota(i32, (1, count), 1)
        places = slot % block_len
        for block in range(ref.shape[0]):
            piece = piece_of + block // shard_blocks
            far, by = piece // head_count, piece % head_count
            physical = ((tok_index ^ far) * head_count + (head_index ^ by)) * shard_blocks
            logical = table[0, physical + block % shard_blocks]
            places = places + jnp.where(slot // block_len == block, logical * block_len, 0)
        piece_of += ref.shape[0] // shard_blocks
        allowed.append((places < SINK) | (places > prefix_len + own_offset - WINDOW))
    attended = attend(
        queries[...],
        jnp.concatenate(keys, axis=0),
        jnp.concatenate(values, axis=0),
        jnp.concatenate([a.astype(i32) for a in allowed], axis=1) != 0,
    )
    share = rows // head_count
    for by, out in enumerate(outs):
        out[...] = jnp.zeros_like(out)
    term = dot(attended, w_out[...]).astype(bf16)
    for owner in range(head_count):
        for by, out in enumerate(outs):

            @pl.when((head_index ^ by) == owner)
            def _(out=out, owner=owner):
                out[...] = term[owner * share : (owner + 1) * share]


def after_self_body(place, tokens, *refs):
    terms, (after, normed) = refs[:-2], refs[-2:]
    share = after.shape[0]
    start = pl.multiple_of(place[1] * share, share)
    total = tokens[0, pl.ds(start, share), :].astype(f32)
    total = total + sum(term[...].astype(f32) for term in terms)
    after[...] = total
    normed[...] = layer_norm(total).astype(bf16)


def cross_body(head_count, w_cross_query, cross_cache, w_cross_out, *refs):
    rows_in, outs = refs[:head_count], refs[head_count:]
    normed = jnp.concatenate([ref[...] for ref in rows_in], axis=0)
    queries = dot(normed, w_cross_query[...]).astype(bf16)
    keys, values = split_pair(cross_cache[0])
    cross_out = attend(queries, keys, values, None)
    term = dot(cross_out, w_cross_out[...]).astype(bf16)
    share = rows_in[0].shape[0]
    for by, out in enumerate(outs):
        out[...] = term[by * share : (by + 1) * share]


def after_cross_body(before, *refs):
    terms, (after, normed) = refs[:-2], refs[-2:]
    total = before[...] + sum(term[...].astype(f32) for term in terms)
    after[...] = total
    normed[...] = layer_norm(total).astype(bf16)


def hidden_body(head_count, w_up, w_down, *refs):
    rows_in, outs = refs[:head_count], refs[head_count:]
    normed = jnp.concatenate([ref[...] for ref in rows_in], axis=0)
    hidden = jax.nn.relu(dot(normed, w_up[...])).astype(bf16)
    term = dot(hidden, w_down[...]).astype(bf16)
    share = rows_in[0].shape[0]
    for by, out in enumerate(outs):
        out[...] = term[by * share : (by + 1) * share]


def on_device(
    tokens,
    lengths,
    block_position,
    prefix_pool,
    cross_cache,
    w_query,
    w_keyvalue,
    w_out,
    w_cross_query,
    w_cross_out,
    w_up,
    w_down,
):
    rows, model_width = tokens.shape[1:]
    width = w_query.shape[1]
    tok_index, head_index = lax.axis_index("tok"), lax.axis_index("head")
    tok_count, head_count = lax.axis_size("tok"), lax.axis_size("head")
    share = rows // head_count
    place = jnp.stack([tok_index, head_index]).astype(i32)
    shape = jax.ShapeDtypeStruct
    row_pieces = [shape((share, model_width), bf16)] * head_count
    stats = [shape((share, model_width), f32), shape((share, model_width), bf16)]

    slots = scatter_heads(
        [
            lax.dynamic_slice_in_dim(prefix_pool[0], (head_index ^ by) * width, width, 3)
            for by in range(head_count)
        ]
    )
    queries, keyvalue = kernel_call(
        project_body,
        [shape((rows, width), bf16), shape((rows, 2 * width), bf16)],
        6 * rows * model_width * width,
        tokens,
        w_query,
        w_keyvalue,
    )
    near = [keyvalue] + [
        from_behind(keyvalue, "tok", distance)
        for distance in range(1, min(SPAN, tok_count - 1) + 1)
    ]
    own_slots = jnp.concatenate(slots, axis=0)
    far_slots = [swap(own_slots, "tok", by) for by in range(1, tok_count)]
    slot_rows = tok_count * own_slots.shape[0] * own_slots.shape[1]
    terms = kernel_call(
        functools.partial(self_body, len(near), head_count, tok_count),
        row_pieces,
        4 * rows * width * (len(near) * rows + slot_rows) + 2 * rows * width * model_width,
        place,
        lengths,
        block_position,
        queries,
        w_out,
        *near,
        *slots,
        *far_slots,
    )
    after_self, normed = kernel_call(
        after_self_body, stats, 0, place, tokens, *scatter_heads(terms)
    )
    terms = kernel_call(
        functools.partial(cross_body, head_count),
        row_pieces,
        4 * rows * model_width * width,
        w_cross_query,
        cross_cache,
        w_cross_out,
        *gather_heads(normed),
    )
    after_cross, normed = kernel_call(
        after_cross_body, stats, 0, after_self, *scatter_heads(terms)
    )
    terms = kernel_call(
        functools.partial(hidden_body, head_count),
        row_pieces,
        4 * rows * model_width * w_up.shape[1],
        w_up,
        w_down,
        *gather_heads(normed),
    )
    result = after_cross + sum(term.astype(f32) for term in scatter_heads(terms))
    return result.astype(bf16)[None]


def solution(mesh):
    return jax.shard_map(
        on_device,
        mesh=mesh,
        in_specs=(
            P("grp", "tok", None),
            P("grp", None),
            P("grp", None),
            P("grp", ("tok", "head"), None, None, None),
            P("grp", None, None, "head"),
            P(None, "head"),
            P(None, None, "head"),
            P("head", None),
            P(None, "head"),
            P("head", None),
            P(None, "head"),
            P("head", None),
        ),
        out_specs=P("grp", ("tok", "head"), None),
        check_vma=False,
    )
```

```python
import functools

import jax
import jax.numpy as jnp
from jax import lax
from jax.experimental import pallas as pl
from jax.experimental.pallas import tpu as pltpu
from jax.sharding import PartitionSpec as P

HEAD_DIM = 64
SPAN = 8
SINK = 4
WINDOW = 1024
SCALE = HEAD_DIM ** (-0.5)
EPS = 1e-05
SMALL_VMEM = 12 << 20
KERNEL_FLOPS = 4 * 10**9
WIDE_SCORES = 8 << 20

bf16 = jnp.bfloat16
f32 = jnp.float32
i32 = jnp.int32


def swap(array, axis, by):
    count = lax.axis_size(axis)
    return lax.ppermute(array, axis, [(i, i ^ by) for i in range(count)])


def from_behind(array, axis, by):
    count = lax.axis_size(axis)
    return lax.ppermute(array, axis, [(i, (i + by) % count) for i in range(count)])


def gather_heads(array):
    return [array] + [swap(array, "head", by) for by in range(1, lax.axis_size("head"))]


def scatter_heads(pieces):
    return [pieces[0]] + [swap(piece, "head", by) for by, piece in enumerate(pieces) if by]


def kernel_call(body, outs, vmem_bytes, scratch, specs, out_specs, *args):
    return pl.pallas_call(
        body,
        out_shape=outs,
        in_specs=list(specs) + [pl.BlockSpec()] * (len(args) - len(specs)),
        out_specs=out_specs or [pl.BlockSpec()] * len(outs),
        scratch_shapes=scratch,
        compiler_params=pltpu.CompilerParams(vmem_limit_bytes=vmem_bytes),
        cost_estimate=pl.CostEstimate(
            flops=KERNEL_FLOPS, bytes_accessed=sum(a.nbytes for a in args), transcendentals=0
        ),
    )(*args)


scalars = pl.BlockSpec(memory_space=pltpu.SMEM)
in_hbm = pl.BlockSpec(memory_space=pltpu.HBM)


def layer_norm(values):
    center = values - jnp.mean(values, axis=-1, keepdims=True)
    spread = jnp.mean(center * center, axis=-1, keepdims=True)
    return center * lax.rsqrt(spread + EPS)


def dot(left, right):
    return jnp.dot(left, right, preferred_element_type=f32)


def split_pair(pairs):
    rows, _, width = pairs.shape
    flat = pairs.astype(f32).reshape(rows, 2 * width).astype(bf16)
    return flat[:, :width], flat[:, width:]


def head_lanes(shape):
    return lax.broadcasted_iota(i32, shape, len(shape) - 1) // HEAD_DIM


def attend_heads(queries, keys, values, bias, heads):
    rows, width = queries.shape
    lanes = head_lanes((rows, width))
    stacked = jnp.concatenate(
        [jnp.where(lanes == h, queries, jnp.zeros_like(queries)) for h in heads], axis=0
    )
    scores = lax.dot_general(
        stacked, keys, (((1,), (1,)), ((), ())), preferred_element_type=f32
    ).reshape(len(heads), rows, keys.shape[0])
    scores = scores * SCALE
    if bias is not None:
        scores = scores + bias[None]
    row_max = jnp.max(scores, axis=-1, keepdims=True)
    weights = jnp.exp(scores - row_max)
    row_sum = jnp.sum(weights, axis=-1, keepdims=True)
    summed = dot(weights.astype(bf16).reshape(len(heads) * rows, -1), values)
    summed = summed.reshape(len(heads), rows, width) / row_sum
    result = jnp.zeros((rows, width), f32)
    for i, h in enumerate(heads):
        result = jnp.where(lanes == h, summed[i], result)
    return result


def attend(queries, keys, values, bias):
    rows, width = queries.shape
    heads = list(range(width // HEAD_DIM))
    if len(heads) * rows * keys.shape[0] * 4 <= WIDE_SCORES:
        return attend_heads(queries, keys, values, bias, heads).astype(bf16)
    result = attend_heads(queries, keys, values, bias, heads[:1])
    for h in heads[1:]:
        result = result + attend_heads(queries, keys, values, bias, [h])
    return result.astype(bf16)


def request_info(token_ids, length_of, requests):
    request = jnp.zeros_like(token_ids)
    first_token = jnp.zeros_like(token_ids)
    end = jnp.int32(0)
    for i in range(requests):
        end = end + length_of(i)
        before = end <= token_ids
        request = request + before.astype(i32)
        first_token = jnp.where(before, first_token + length_of(i), first_token)
    return request, token_ids - first_token


def columns_body(place, pool, *outs):
    width = outs[0].shape[-1]
    for by, out in enumerate(outs):
        first = pl.multiple_of((place[1] ^ by) * width, width)
        out[...] = pool[0, :, :, :, pl.ds(first, width)]


def project_body(
    sizes, place, lengths_in, table_in, tokens, w_query, w_keyvalue, queries, keyvalue, bias, residual,
    lengths, table, sems,
):
    near, tok_count, head_count, shard_blocks, block_len = sizes
    requests = lengths.shape[1]
    copies = [
        pltpu.make_async_copy(lengths_in, lengths, sems.at[0]),
        pltpu.make_async_copy(table_in, table, sems.at[1]),
    ]
    for copy in copies:
        copy.start()
    normed = layer_norm(tokens[0].astype(f32)).astype(bf16)
    queries[...] = dot(normed, w_query[...]).astype(bf16)
    w_key, w_value = split_pair(w_keyvalue[...])
    rows, width = queries.shape
    keyvalue[:, :width] = dot(normed, w_key).astype(bf16)
    keyvalue[:, width:] = dot(normed, w_value).astype(bf16)

    for copy in copies:
        copy.wait()
    tok_index, head_index = place[0], place[1]
    share = residual.shape[0]
    start = pl.multiple_of(head_index * share, share)
    residual[...] = tokens[0, pl.ds(start, share), :].astype(f32)

    def length_of(i):
        return lengths[0, i]

    own_ids = tok_index * rows + lax.broadcasted_iota(i32, (rows, 1), 0)
    own_request, own_offset = request_info(own_ids, length_of, requests)
    for distance in range(near):
        ids = (tok_index - distance) * rows + lax.broadcasted_iota(i32, (1, rows), 1)
        allowed = (
            (ids >= 0)
            & (request_info(ids, length_of, requests)[0] == own_request)
            & (ids <= own_ids)
            & (own_ids - ids < WINDOW)
        )
        bias[:, distance * rows : (distance + 1) * rows] = jnp.where(allowed, 0.0, -jnp.inf)
    shard = head_count * shard_blocks * block_len
    prefix_len = tok_count * shard
    slot = lax.broadcasted_iota(i32, (1, shard), 1)
    for far in range(tok_count):
        places = slot % block_len
        for block in range(head_count * shard_blocks):
            owner = (tok_index ^ far) * head_count + (head_index ^ (block // shard_blocks))
            logical = table[0, owner * shard_blocks + block % shard_blocks]
            places = places + jnp.where(slot // block_len == block, logical * block_len, 0)
        allowed = (places < SINK) | (places > prefix_len + own_offset - WINDOW)
        first = near * rows + far * shard
        bias[:, first : first + shard] = jnp.where(allowed, 0.0, -jnp.inf)


def self_body(near, head_count, place, queries, bias, w_out, *refs):
    term, refs = refs[-1], refs[:-1]
    near_refs, refs = refs[:near], refs[near:]
    slot_refs, outs = refs[:-head_count], refs[-head_count:]
    rows, width = queries.shape
    keys = [ref[:, :width] for ref in near_refs]
    values = [ref[:, width:] for ref in near_refs]
    for ref in slot_refs:
        key, value = split_pair(ref[...].reshape(ref.shape[0] * ref.shape[1], 2, width))
        keys.append(key)
        values.append(value)
    attended = attend(
        queries[...], jnp.concatenate(keys, axis=0), jnp.concatenate(values, axis=0), bias[...]
    )
    share = rows // head_count
    term[...] = dot(attended, w_out[...]).astype(bf16)
    for by, out in enumerate(outs):
        start = pl.multiple_of((place[1] ^ by) * share, share)
        out[...] = term[pl.ds(start, share), :]


def cross_body(head_count, w_cross_query, cross_cache, w_cross_out, *refs):
    rows_in, outs = refs[:head_count], refs[head_count:]
    normed = jnp.concatenate([ref[...] for ref in rows_in], axis=0)
    queries = dot(normed, w_cross_query[...]).astype(bf16)
    keys, values = split_pair(cross_cache[0])
    cross_out = attend(queries, keys, values, None)
    term = dot(cross_out, w_cross_out[...]).astype(bf16)
    share = rows_in[0].shape[0]
    for by, out in enumerate(outs):
        out[...] = term[by * share : (by + 1) * share]


def after_body(before, *refs):
    terms, (after, normed) = refs[:-2], refs[-2:]
    total = before[...] + sum(term[...].astype(f32) for term in terms)
    after[...] = total
    normed[...] = layer_norm(total).astype(bf16)


def hidden_body(head_count, w_up, w_down, *refs):
    rows_in, outs = refs[:head_count], refs[head_count:]
    normed = jnp.concatenate([ref[...] for ref in rows_in], axis=0)
    hidden = jax.nn.relu(dot(normed, w_up[...])).astype(bf16)
    term = dot(hidden, w_down[...]).astype(bf16)
    share = rows_in[0].shape[0]
    for by, out in enumerate(outs):
        out[...] = term[by * share : (by + 1) * share]


def on_device(
    tokens,
    lengths,
    block_position,
    prefix_pool,
    cross_cache,
    w_query,
    w_keyvalue,
    w_out,
    w_cross_query,
    w_cross_out,
    w_up,
    w_down,
):
    rows, model_width = tokens.shape[1:]
    width = w_query.shape[1]
    tok_index, head_index = lax.axis_index("tok"), lax.axis_index("head")
    tok_count, head_count = lax.axis_size("tok"), lax.axis_size("head")
    share = rows // head_count
    place = jnp.stack([tok_index, head_index]).astype(i32)
    shard_blocks, block_len = prefix_pool.shape[1:3]
    near_count = 1 + min(SPAN, tok_count - 1)
    key_count = near_count * rows + block_position.shape[1] * block_len
    sizes = (near_count, tok_count, head_count, shard_blocks, block_len)
    shape = jax.ShapeDtypeStruct
    row_pieces = [shape((share, model_width), bf16)] * head_count
    stats = [shape((share, model_width), f32), shape((share, model_width), bf16)]

    pool_columns = kernel_call(
        columns_body,
        [shape((shard_blocks, block_len, 2, width), bf16)] * head_count,
        SMALL_VMEM,
        [],
        [scalars],
        None,
        place,
        prefix_pool,
    )
    slots = scatter_heads(pool_columns)
    queries, keyvalue, bias, residual = kernel_call(
        functools.partial(project_body, sizes),
        [
            shape((rows, width), bf16),
            shape((rows, 2 * width), bf16),
            shape((rows, key_count), f32),
            shape((share, model_width), f32),
        ],
        2 * SMALL_VMEM,
        [
            pltpu.SMEM(lengths.shape, i32),
            pltpu.SMEM(block_position.shape, i32),
            pltpu.SemaphoreType.DMA((2,)),
        ],
        [scalars, in_hbm, in_hbm],
        None,
        place,
        lengths,
        block_position,
        tokens,
        w_query,
        w_keyvalue,
    )
    near = [keyvalue] + [
        from_behind(keyvalue, "tok", distance) for distance in range(1, near_count)
    ]
    all_slots = list(slots)
    for by in range(1, tok_count):
        for piece in slots:
            all_slots.append(swap(lax.optimization_barrier((piece, keyvalue))[0], "tok", by))
    terms = kernel_call(
        functools.partial(self_body, near_count, head_count),
        row_pieces,
        SMALL_VMEM + 36 * rows * key_count,
        [pltpu.VMEM((rows, model_width), bf16)],
        [scalars],
        None,
        place,
        queries,
        bias,
        w_out,
        *near,
        *all_slots,
    )
    after_self, normed = kernel_call(
        after_body, stats, SMALL_VMEM, [], [], None, residual, *scatter_heads(terms)
    )
    terms = kernel_call(
        functools.partial(cross_body, head_count),
        row_pieces,
        SMALL_VMEM,
        [],
        [],
        None,
        w_cross_query,
        cross_cache,
        w_cross_out,
        *gather_heads(normed),
    )
    after_cross, normed = kernel_call(
        after_body, stats, SMALL_VMEM, [], [], None, after_self, *scatter_heads(terms)
    )
    terms = kernel_call(
        functools.partial(hidden_body, head_count),
        row_pieces,
        2 * SMALL_VMEM,
        [],
        [],
        None,
        w_up,
        w_down,
        *gather_heads(normed),
    )
    result = after_cross + sum(term.astype(f32) for term in scatter_heads(terms))
    return result.astype(bf16)[None]


def solution(mesh):
    return jax.shard_map(
        on_device,
        mesh=mesh,
        in_specs=(
            P("grp", "tok", None),
            P("grp", None),
            P("grp", None),
            P("grp", ("tok", "head"), None, None, None),
            P("grp", None, None, "head"),
            P(None, "head"),
            P(None, None, "head"),
            P("head", None),
            P(None, "head"),
            P("head", None),
            P(None, "head"),
            P("head", None),
        ),
        out_specs=P("grp", ("tok", "head"), None),
        check_vma=False,
    )
```

```python
import functools

import jax
import jax.numpy as jnp
from jax import lax
from jax.experimental import pallas as pl
from jax.experimental.pallas import tpu as pltpu
from jax.sharding import PartitionSpec as P

HEAD_DIM = 64
SPAN = 8
SINK = 4
WINDOW = 1024
SCALE = HEAD_DIM ** (-0.5)
EPS = 1e-05
SMALL_VMEM = 12 << 20
KERNEL_FLOPS = 4 * 10**9
WIDE_SCORES = 8 << 20

bf16 = jnp.bfloat16
f32 = jnp.float32
i32 = jnp.int32


def swap(array, axis, by):
    count = lax.axis_size(axis)
    return lax.ppermute(array, axis, [(i, i ^ by) for i in range(count)])


def from_behind(array, axis, by):
    count = lax.axis_size(axis)
    return lax.ppermute(array, axis, [(i, (i + by) % count) for i in range(count)])


def rounds(count):
    return [0, count // 2] + [by for by in range(1, count) if by != count // 2]


def arrivals(count):
    own, *others = rounds(count)
    return [own] + others[::-1]


def rotate(array, by):
    return array if by == 0 else from_behind(array, "head", by)


def gather_heads(array):
    return [rotate(array, by) for by in arrivals(lax.axis_size("head"))]


def scatter_heads(pieces):
    return [rotate(piece, by) for piece, by in zip(pieces, rounds(len(pieces)))]


def ahead(head_index, by, count):
    return lax.rem(head_index + by + count, count)


def kernel_call(body, outs, vmem_bytes, scratch, specs, out_specs, *args):
    return pl.pallas_call(
        body,
        out_shape=outs,
        in_specs=list(specs) + [pl.BlockSpec()] * (len(args) - len(specs)),
        out_specs=out_specs or [pl.BlockSpec()] * len(outs),
        scratch_shapes=scratch,
        compiler_params=pltpu.CompilerParams(vmem_limit_bytes=vmem_bytes),
        cost_estimate=pl.CostEstimate(
            flops=KERNEL_FLOPS, bytes_accessed=sum(a.nbytes for a in args), transcendentals=0
        ),
    )(*args)


scalars = pl.BlockSpec(memory_space=pltpu.SMEM)
in_hbm = pl.BlockSpec(memory_space=pltpu.HBM)


def layer_norm(values):
    center = values - jnp.mean(values, axis=-1, keepdims=True)
    spread = jnp.mean(center * center, axis=-1, keepdims=True)
    return center * lax.rsqrt(spread + EPS)


def dot(left, right):
    return jnp.dot(left, right, preferred_element_type=f32)


def split_pair(pairs):
    rows, _, width = pairs.shape
    flat = pairs.astype(f32).reshape(rows, 2 * width).astype(bf16)
    return flat[:, :width], flat[:, width:]


def head_lanes(shape):
    return lax.broadcasted_iota(i32, shape, len(shape) - 1) // HEAD_DIM


def attend_heads(queries, keys, values, bias, heads):
    rows, width = queries.shape
    lanes = head_lanes((rows, width))
    stacked = jnp.concatenate(
        [jnp.where(lanes == h, queries, jnp.zeros_like(queries)) for h in heads], axis=0
    )
    scores = lax.dot_general(
        stacked, keys, (((1,), (1,)), ((), ())), preferred_element_type=f32
    ).reshape(len(heads), rows, keys.shape[0])
    scores = scores * SCALE
    if bias is not None:
        scores = scores + bias[None]
    row_max = jnp.max(scores, axis=-1, keepdims=True)
    weights = jnp.exp(scores - row_max)
    row_sum = jnp.sum(weights, axis=-1, keepdims=True)
    summed = dot(weights.astype(bf16).reshape(len(heads) * rows, -1), values)
    summed = summed.reshape(len(heads), rows, width) / row_sum
    result = jnp.zeros((rows, width), f32)
    for i, h in enumerate(heads):
        result = jnp.where(lanes == h, summed[i], result)
    return result


def attend(queries, keys, values, bias):
    rows, width = queries.shape
    heads = list(range(width // HEAD_DIM))
    if len(heads) * rows * keys.shape[0] * 4 <= WIDE_SCORES:
        return attend_heads(queries, keys, values, bias, heads).astype(bf16)
    result = attend_heads(queries, keys, values, bias, heads[:1])
    for h in heads[1:]:
        result = result + attend_heads(queries, keys, values, bias, [h])
    return result.astype(bf16)


def request_info(token_ids, length_of, requests):
    request = jnp.zeros_like(token_ids)
    first_token = jnp.zeros_like(token_ids)
    end = jnp.int32(0)
    for i in range(requests):
        end = end + length_of(i)
        before = end <= token_ids
        request = request + before.astype(i32)
        first_token = jnp.where(before, first_token + length_of(i), first_token)
    return request, token_ids - first_token


def columns_body(place, pool, *outs):
    width = outs[0].shape[-1]
    for by, out in zip(rounds(len(outs)), outs):
        first = pl.multiple_of(ahead(place[1], by, len(outs)) * width, width)
        out[...] = pool[0, :, :, :, pl.ds(first, width)]


def project_body(
    sizes, place, lengths_in, table_in, tokens, w_query, w_keyvalue, queries, keyvalue, bias, residual,
    lengths, table, sems,
):
    near, tok_count, head_count, shard_blocks, block_len = sizes
    requests = lengths.shape[1]
    copies = [
        pltpu.make_async_copy(lengths_in, lengths, sems.at[0]),
        pltpu.make_async_copy(table_in, table, sems.at[1]),
    ]
    for copy in copies:
        copy.start()
    normed = layer_norm(tokens[0].astype(f32)).astype(bf16)
    queries[...] = dot(normed, w_query[...]).astype(bf16)
    w_key, w_value = split_pair(w_keyvalue[...])
    rows, width = queries.shape
    keyvalue[:, :width] = dot(normed, w_key).astype(bf16)
    keyvalue[:, width:] = dot(normed, w_value).astype(bf16)

    for copy in copies:
        copy.wait()
    tok_index, head_index = place[0], place[1]
    share = residual.shape[0]
    start = pl.multiple_of(head_index * share, share)
    residual[...] = tokens[0, pl.ds(start, share), :].astype(f32)

    def length_of(i):
        return lengths[0, i]

    own_ids = tok_index * rows + lax.broadcasted_iota(i32, (rows, 1), 0)
    own_request, own_offset = request_info(own_ids, length_of, requests)
    for distance in range(near):
        ids = (tok_index - distance) * rows + lax.broadcasted_iota(i32, (1, rows), 1)
        allowed = (
            (ids >= 0)
            & (request_info(ids, length_of, requests)[0] == own_request)
            & (ids <= own_ids)
            & (own_ids - ids < WINDOW)
        )
        bias[:, distance * rows : (distance + 1) * rows] = jnp.where(allowed, 0.0, -jnp.inf)
    shard = head_count * shard_blocks * block_len
    prefix_len = tok_count * shard
    slot = lax.broadcasted_iota(i32, (1, shard), 1)
    for far in range(tok_count):
        places = slot % block_len
        for block in range(head_count * shard_blocks):
            owner = (tok_index ^ far) * head_count + ahead(
                head_index, -rounds(head_count)[block // shard_blocks], head_count
            )
            logical = table[0, owner * shard_blocks + block % shard_blocks]
            places = places + jnp.where(slot // block_len == block, logical * block_len, 0)
        allowed = (places < SINK) | (places > prefix_len + own_offset - WINDOW)
        first = near * rows + far * shard
        bias[:, first : first + shard] = jnp.where(allowed, 0.0, -jnp.inf)


def self_body(near, head_count, place, queries, bias, w_out, *refs):
    term, refs = refs[-1], refs[:-1]
    near_refs, refs = refs[:near], refs[near:]
    slot_refs, outs = refs[:-head_count], refs[-head_count:]
    rows, width = queries.shape
    keys = [ref[:, :width] for ref in near_refs]
    values = [ref[:, width:] for ref in near_refs]
    for ref in slot_refs:
        key, value = split_pair(ref[...].reshape(ref.shape[0] * ref.shape[1], 2, width))
        keys.append(key)
        values.append(value)
    attended = attend(
        queries[...], jnp.concatenate(keys, axis=0), jnp.concatenate(values, axis=0), bias[...]
    )
    share = rows // head_count
    term[...] = dot(attended, w_out[...]).astype(bf16)
    for by, out in zip(rounds(head_count), outs):
        start = pl.multiple_of(ahead(place[1], by, head_count) * share, share)
        out[...] = term[pl.ds(start, share), :]


def cross_body(head_count, w_cross_query, cross_cache, w_cross_out, *refs):
    rows_in, outs = refs[:head_count], refs[head_count:]
    normed = jnp.concatenate([ref[...] for ref in rows_in], axis=0)
    queries = dot(normed, w_cross_query[...]).astype(bf16)
    keys, values = split_pair(cross_cache[0])
    cross_out = attend(queries, keys, values, None)
    term = dot(cross_out, w_cross_out[...]).astype(bf16)
    share = rows_in[0].shape[0]
    for by, out in zip(rounds(head_count), outs):
        row = arrivals(head_count).index(-by % head_count)
        out[...] = term[row * share : (row + 1) * share]


def after_body(before, *refs):
    terms, (after, normed) = refs[:-2], refs[-2:]
    total = before[...] + sum(term[...].astype(f32) for term in terms)
    after[...] = total
    normed[...] = layer_norm(total).astype(bf16)


def hidden_body(head_count, w_up, w_down, *refs):
    rows_in, outs = refs[:head_count], refs[head_count:]
    normed = jnp.concatenate([ref[...] for ref in rows_in], axis=0)
    hidden = jax.nn.relu(dot(normed, w_up[...])).astype(bf16)
    term = dot(hidden, w_down[...]).astype(bf16)
    share = rows_in[0].shape[0]
    for by, out in zip(rounds(head_count), outs):
        row = arrivals(head_count).index(-by % head_count)
        out[...] = term[row * share : (row + 1) * share]


def on_device(
    tokens,
    lengths,
    block_position,
    prefix_pool,
    cross_cache,
    w_query,
    w_keyvalue,
    w_out,
    w_cross_query,
    w_cross_out,
    w_up,
    w_down,
):
    rows, model_width = tokens.shape[1:]
    width = w_query.shape[1]
    tok_index, head_index = lax.axis_index("tok"), lax.axis_index("head")
    tok_count, head_count = lax.axis_size("tok"), lax.axis_size("head")
    share = rows // head_count
    place = jnp.stack([tok_index, head_index]).astype(i32)
    shard_blocks, block_len = prefix_pool.shape[1:3]
    near_count = 1 + min(SPAN, tok_count - 1)
    key_count = near_count * rows + block_position.shape[1] * block_len
    sizes = (near_count, tok_count, head_count, shard_blocks, block_len)
    shape = jax.ShapeDtypeStruct
    row_pieces = [shape((share, model_width), bf16)] * head_count
    stats = [shape((share, model_width), f32), shape((share, model_width), bf16)]

    pool_columns = kernel_call(
        columns_body,
        [shape((shard_blocks, block_len, 2, width), bf16)] * head_count,
        SMALL_VMEM,
        [],
        [scalars],
        None,
        place,
        prefix_pool,
    )
    slots = scatter_heads(pool_columns)
    queries, keyvalue, bias, residual = kernel_call(
        functools.partial(project_body, sizes),
        [
            shape((rows, width), bf16),
            shape((rows, 2 * width), bf16),
            shape((rows, key_count), f32),
            shape((share, model_width), f32),
        ],
        2 * SMALL_VMEM,
        [
            pltpu.SMEM(lengths.shape, i32),
            pltpu.SMEM(block_position.shape, i32),
            pltpu.SemaphoreType.DMA((2,)),
        ],
        [scalars, in_hbm, in_hbm],
        None,
        place,
        lengths,
        block_position,
        tokens,
        w_query,
        w_keyvalue,
    )
    near = [keyvalue] + [
        from_behind(keyvalue, "tok", distance) for distance in range(1, near_count)
    ]
    all_slots = list(slots)
    for by in range(1, tok_count):
        for piece in slots:
            all_slots.append(swap(lax.optimization_barrier((piece, keyvalue))[0], "tok", by))
    terms = kernel_call(
        functools.partial(self_body, near_count, head_count),
        row_pieces,
        SMALL_VMEM + 36 * rows * key_count,
        [pltpu.VMEM((rows, model_width), bf16)],
        [scalars],
        None,
        place,
        queries,
        bias,
        w_out,
        *near,
        *all_slots,
    )
    after_self, normed = kernel_call(
        after_body, stats, SMALL_VMEM, [], [], None, residual, *scatter_heads(terms)
    )
    terms = kernel_call(
        functools.partial(cross_body, head_count),
        row_pieces,
        SMALL_VMEM,
        [],
        [],
        None,
        w_cross_query,
        cross_cache,
        w_cross_out,
        *gather_heads(normed),
    )
    after_cross, normed = kernel_call(
        after_body, stats, SMALL_VMEM, [], [], None, after_self, *scatter_heads(terms)
    )
    terms = kernel_call(
        functools.partial(hidden_body, head_count),
        row_pieces,
        2 * SMALL_VMEM,
        [],
        [],
        None,
        w_up,
        w_down,
        *gather_heads(normed),
    )
    result = after_cross + sum(term.astype(f32) for term in scatter_heads(terms))
    return result.astype(bf16)[None]


def solution(mesh):
    return jax.shard_map(
        on_device,
        mesh=mesh,
        in_specs=(
            P("grp", "tok", None),
            P("grp", None),
            P("grp", None),
            P("grp", ("tok", "head"), None, None, None),
            P("grp", None, None, "head"),
            P(None, "head"),
            P(None, None, "head"),
            P("head", None),
            P(None, "head"),
            P("head", None),
            P(None, "head"),
            P("head", None),
        ),
        out_specs=P("grp", ("tok", "head"), None),
        check_vma=False,
    )
```

```python
import functools

import jax
import jax.numpy as jnp
from jax import lax
from jax.experimental import pallas as pl
from jax.experimental.pallas import tpu as pltpu
from jax.sharding import PartitionSpec as P

HEAD_DIM = 64
SPAN = 8
SINK = 4
WINDOW = 1024
SCALE = HEAD_DIM ** (-0.5)
EPS = 1e-05
SMALL_VMEM = 12 << 20
KERNEL_FLOPS = 4 * 10**9
WIDE_SCORES = 8 << 20

bf16 = jnp.bfloat16
f32 = jnp.float32
i32 = jnp.int32


def swap(array, axis, by):
    count = lax.axis_size(axis)
    return lax.ppermute(array, axis, [(i, i ^ by) for i in range(count)])


def from_behind(array, axis, by):
    count = lax.axis_size(axis)
    return lax.ppermute(array, axis, [(i, (i + by) % count) for i in range(count)])


def rounds(count):
    return [0, count // 2] + [by for by in range(1, count) if by != count // 2]


def rotate(array, by):
    return array if by == 0 else from_behind(array, "head", by)


def exchange_heads(pieces):
    return [rotate(piece, by) for piece, by in zip(pieces, rounds(len(pieces)))]


def ahead(by, count):
    return lax.rem(lax.axis_index("head") + by + count, count)


def kernel_call(body, outs, vmem_bytes, scratch, specs, out_specs, *args):
    return pl.pallas_call(
        body,
        out_shape=outs,
        in_specs=list(specs) + [pl.BlockSpec()] * (len(args) - len(specs)),
        out_specs=out_specs or [pl.BlockSpec()] * len(outs),
        scratch_shapes=scratch,
        compiler_params=pltpu.CompilerParams(vmem_limit_bytes=vmem_bytes),
        cost_estimate=pl.CostEstimate(
            flops=KERNEL_FLOPS, bytes_accessed=sum(a.nbytes for a in args), transcendentals=0
        ),
    )(*args)


in_hbm = pl.BlockSpec(memory_space=pltpu.HBM)


def layer_norm(values):
    center = values - jnp.mean(values, axis=-1, keepdims=True)
    spread = jnp.mean(center * center, axis=-1, keepdims=True)
    return center * lax.rsqrt(spread + EPS)


def dot(left, right):
    return jnp.dot(left, right, preferred_element_type=f32)


def split_pair(pairs):
    rows, _, width = pairs.shape
    flat = pairs.astype(f32).reshape(rows, 2 * width).astype(bf16)
    return flat[:, :width], flat[:, width:]


def head_lanes(shape):
    return lax.broadcasted_iota(i32, shape, len(shape) - 1) // HEAD_DIM


def attend_heads(queries, keys, values, bias, heads):
    rows, width = queries.shape
    lanes = head_lanes((rows, width))
    stacked = jnp.concatenate(
        [jnp.where(lanes == h, queries, jnp.zeros_like(queries)) for h in heads], axis=0
    )
    scores = lax.dot_general(
        stacked, keys, (((1,), (1,)), ((), ())), preferred_element_type=f32
    ).reshape(len(heads), rows, keys.shape[0])
    scores = scores * SCALE
    if bias is not None:
        scores = scores + bias[None]
    row_max = jnp.max(scores, axis=-1, keepdims=True)
    weights = jnp.exp(scores - row_max)
    row_sum = jnp.sum(weights, axis=-1, keepdims=True)
    summed = dot(weights.astype(bf16).reshape(len(heads) * rows, -1), values)
    summed = summed.reshape(len(heads), rows, width) / row_sum
    result = jnp.zeros((rows, width), f32)
    for i, h in enumerate(heads):
        result = jnp.where(lanes == h, summed[i], result)
    return result


def attend(queries, keys, values, bias):
    rows, width = queries.shape
    heads = list(range(width // HEAD_DIM))
    if len(heads) * rows * keys.shape[0] * 4 <= WIDE_SCORES:
        return attend_heads(queries, keys, values, bias, heads).astype(bf16)
    result = attend_heads(queries, keys, values, bias, heads[:1])
    for h in heads[1:]:
        result = result + attend_heads(queries, keys, values, bias, [h])
    return result.astype(bf16)


def request_info(token_ids, length_of, requests):
    request = jnp.zeros_like(token_ids)
    first_token = jnp.zeros_like(token_ids)
    end = jnp.int32(0)
    for i in range(requests):
        end = end + length_of(i)
        before = end <= token_ids
        request = request + before.astype(i32)
        first_token = jnp.where(before, first_token + length_of(i), first_token)
    return request, token_ids - first_token


def columns_body(pool, *outs):
    width = outs[0].shape[-1]
    for by, out in zip(rounds(len(outs)), outs):
        first = pl.multiple_of(ahead(by, len(outs)) * width, width)
        out[...] = pool[0, :, :, :, pl.ds(first, width)]


def project_body(
    sizes, lengths_in, table_in, tokens, w_query, w_keyvalue, queries, keyvalue, bias, residual,
    lengths, table, sems,
):
    near, tok_count, head_count, shard_blocks, block_len = sizes
    requests = lengths.shape[1]
    copies = [
        pltpu.make_async_copy(lengths_in, lengths, sems.at[0]),
        pltpu.make_async_copy(table_in, table, sems.at[1]),
    ]
    for copy in copies:
        copy.start()
    normed = layer_norm(tokens[0].astype(f32)).astype(bf16)
    queries[...] = dot(normed, w_query[...]).astype(bf16)
    w_key, w_value = split_pair(w_keyvalue[...])
    rows, width = queries.shape
    keyvalue[:, :width] = dot(normed, w_key).astype(bf16)
    keyvalue[:, width:] = dot(normed, w_value).astype(bf16)

    for copy in copies:
        copy.wait()
    tok_index, head_index = lax.axis_index("tok"), lax.axis_index("head")
    share = residual.shape[0]
    start = pl.multiple_of(head_index * share, share)
    residual[...] = tokens[0, pl.ds(start, share), :].astype(f32)

    def length_of(i):
        return lengths[0, i]

    own_ids = tok_index * rows + lax.broadcasted_iota(i32, (rows, 1), 0)
    own_request, own_offset = request_info(own_ids, length_of, requests)
    for distance in range(near):
        ids = (tok_index - distance) * rows + lax.broadcasted_iota(i32, (1, rows), 1)
        allowed = (
            (ids >= 0)
            & (request_info(ids, length_of, requests)[0] == own_request)
            & (ids <= own_ids)
            & (own_ids - ids < WINDOW)
        )
        bias[:, distance * rows : (distance + 1) * rows] = jnp.where(allowed, 0.0, -jnp.inf)
    shard = head_count * shard_blocks * block_len
    prefix_len = tok_count * shard
    slot = lax.broadcasted_iota(i32, (1, shard), 1)
    for far in range(tok_count):
        places = slot % block_len
        for block in range(head_count * shard_blocks):
            owner = (tok_index ^ far) * head_count + ahead(
                -rounds(head_count)[block // shard_blocks], head_count
            )
            logical = table[0, owner * shard_blocks + block % shard_blocks]
            places = places + jnp.where(slot // block_len == block, logical * block_len, 0)
        allowed = (places < SINK) | (places > prefix_len + own_offset - WINDOW)
        first = near * rows + far * shard
        bias[:, first : first + shard] = jnp.where(allowed, 0.0, -jnp.inf)


def self_body(near, head_count, queries, bias, w_out, *refs):
    term, refs = refs[-1], refs[:-1]
    near_refs, refs = refs[:near], refs[near:]
    slot_refs, outs = refs[:-head_count], refs[-head_count:]
    rows, width = queries.shape
    keys = [ref[:, :width] for ref in near_refs]
    values = [ref[:, width:] for ref in near_refs]
    for ref in slot_refs:
        key, value = split_pair(ref[...].reshape(ref.shape[0] * ref.shape[1], 2, width))
        keys.append(key)
        values.append(value)
    attended = attend(
        queries[...], jnp.concatenate(keys, axis=0), jnp.concatenate(values, axis=0), bias[...]
    )
    share = rows // head_count
    term[...] = dot(attended, w_out[...]).astype(bf16)
    for by, out in zip(rounds(head_count), outs):
        start = pl.multiple_of(ahead(by, head_count) * share, share)
        out[...] = term[pl.ds(start, share), :]


def cross_body(head_count, w_cross_query, cross_cache, w_cross_out, *refs):
    rows_in, outs = refs[:head_count], refs[head_count:]
    normed = jnp.concatenate([ref[...] for ref in rows_in], axis=0)
    queries = dot(normed, w_cross_query[...]).astype(bf16)
    keys, values = split_pair(cross_cache[0])
    cross_out = attend(queries, keys, values, None)
    term = dot(cross_out, w_cross_out[...]).astype(bf16)
    share = rows_in[0].shape[0]
    for by, out in zip(rounds(head_count), outs):
        row = rounds(head_count).index(-by % head_count)
        out[...] = term[row * share : (row + 1) * share]


def after_body(head_count, before, *refs):
    terms, (after, *outs) = refs[:head_count], refs[head_count:]
    total = before[...] + sum(term[...].astype(f32) for term in terms)
    after[...] = total
    normed = layer_norm(total).astype(bf16)
    for out in outs:
        out[...] = normed


def hidden_body(head_count, w_up, w_down, *refs):
    rows_in, outs = refs[:head_count], refs[head_count:]
    normed = jnp.concatenate([ref[...] for ref in rows_in], axis=0)
    hidden = jax.nn.relu(dot(normed, w_up[...])).astype(bf16)
    term = dot(hidden, w_down[...]).astype(bf16)
    share = rows_in[0].shape[0]
    for by, out in zip(rounds(head_count), outs):
        row = rounds(head_count).index(-by % head_count)
        out[...] = term[row * share : (row + 1) * share]


def on_device(
    tokens,
    lengths,
    block_position,
    prefix_pool,
    cross_cache,
    w_query,
    w_keyvalue,
    w_out,
    w_cross_query,
    w_cross_out,
    w_up,
    w_down,
):
    rows, model_width = tokens.shape[1:]
    width = w_query.shape[1]
    tok_count, head_count = lax.axis_size("tok"), lax.axis_size("head")
    share = rows // head_count
    shard_blocks, block_len = prefix_pool.shape[1:3]
    near_count = 1 + min(SPAN, tok_count - 1)
    key_count = near_count * rows + block_position.shape[1] * block_len
    sizes = (near_count, tok_count, head_count, shard_blocks, block_len)
    shape = jax.ShapeDtypeStruct
    row_pieces = [shape((share, model_width), bf16)] * head_count
    stats = [shape((share, model_width), f32)] + row_pieces

    pool_columns = kernel_call(
        columns_body,
        [shape((shard_blocks, block_len, 2, width), bf16)] * head_count,
        SMALL_VMEM,
        [],
        [],
        None,
        prefix_pool,
    )
    slots = exchange_heads(pool_columns)
    queries, keyvalue, bias, residual = kernel_call(
        functools.partial(project_body, sizes),
        [
            shape((rows, width), bf16),
            shape((rows, 2 * width), bf16),
            shape((rows, key_count), f32),
            shape((share, model_width), f32),
        ],
        2 * SMALL_VMEM,
        [
            pltpu.SMEM(lengths.shape, i32),
            pltpu.SMEM(block_position.shape, i32),
            pltpu.SemaphoreType.DMA((2,)),
        ],
        [in_hbm, in_hbm],
        None,
        lengths,
        block_position,
        tokens,
        w_query,
        w_keyvalue,
    )
    near = [keyvalue] + [
        from_behind(keyvalue, "tok", distance) for distance in range(1, near_count)
    ]
    all_slots = list(slots)
    for by in range(1, tok_count):
        for piece in slots:
            all_slots.append(swap(lax.optimization_barrier((piece, keyvalue))[0], "tok", by))
    terms = kernel_call(
        functools.partial(self_body, near_count, head_count),
        row_pieces,
        SMALL_VMEM + 36 * rows * key_count,
        [pltpu.VMEM((rows, model_width), bf16)],
        [],
        None,
        queries,
        bias,
        w_out,
        *near,
        *all_slots,
    )
    after_self, *normed = kernel_call(
        functools.partial(after_body, head_count), stats, SMALL_VMEM, [], [], None, residual, *exchange_heads(terms)
    )
    terms = kernel_call(
        functools.partial(cross_body, head_count),
        row_pieces,
        SMALL_VMEM,
        [],
        [],
        None,
        w_cross_query,
        cross_cache,
        w_cross_out,
        *exchange_heads(normed),
    )
    after_cross, *normed = kernel_call(
        functools.partial(after_body, head_count), stats, SMALL_VMEM, [], [], None, after_self, *exchange_heads(terms)
    )
    terms = kernel_call(
        functools.partial(hidden_body, head_count),
        row_pieces,
        2 * SMALL_VMEM,
        [],
        [],
        None,
        w_up,
        w_down,
        *exchange_heads(normed),
    )
    result = after_cross + sum(term.astype(f32) for term in exchange_heads(terms))
    return result.astype(bf16)[None]


def solution(mesh):
    return jax.shard_map(
        on_device,
        mesh=mesh,
        in_specs=(
            P("grp", "tok", None),
            P("grp", None),
            P("grp", None),
            P("grp", ("tok", "head"), None, None, None),
            P("grp", None, None, "head"),
            P(None, "head"),
            P(None, None, "head"),
            P("head", None),
            P(None, "head"),
            P("head", None),
            P(None, "head"),
            P("head", None),
        ),
        out_specs=P("grp", ("tok", "head"), None),
        check_vma=False,
    )
```

```python
import functools

import jax
import jax.numpy as jnp
from jax import lax
from jax.experimental import pallas as pl
from jax.experimental.pallas import tpu as pltpu
from jax.sharding import PartitionSpec as P

HEAD_DIM = 64
SPAN = 8
SINK = 4
WINDOW = 1024
SCALE = HEAD_DIM ** (-0.5)
EPS = 1e-05
SMALL_VMEM = 12 << 20
KERNEL_FLOPS = 4 * 10**9
WIDE_SCORES = 8 << 20
FULL_ROWS = 128

bf16 = jnp.bfloat16
f32 = jnp.float32
i32 = jnp.int32


def swap(array, axis, by):
    count = lax.axis_size(axis)
    return lax.ppermute(array, axis, [(i, i ^ by) for i in range(count)])


def from_behind(array, axis, by):
    count = lax.axis_size(axis)
    return lax.ppermute(array, axis, [(i, (i + by) % count) for i in range(count)])


def rounds(count):
    return [0, count - 1, *range(1, count - 1)]


def exchange_heads(pieces):
    return [pieces[0]] + [swap(p, "head", by) for p, by in zip(pieces[1:], rounds(len(pieces))[1:])]


def partner(by):
    return lax.axis_index("head") ^ by


def kernel_call(body, outs, vmem_bytes, scratch, specs, out_specs, *args):
    return pl.pallas_call(
        body,
        out_shape=outs,
        in_specs=list(specs) + [pl.BlockSpec()] * (len(args) - len(specs)),
        out_specs=out_specs or [pl.BlockSpec()] * len(outs),
        scratch_shapes=scratch,
        compiler_params=pltpu.CompilerParams(vmem_limit_bytes=vmem_bytes),
        cost_estimate=pl.CostEstimate(
            flops=KERNEL_FLOPS, bytes_accessed=sum(a.nbytes for a in args), transcendentals=0
        ),
    )(*args)


in_hbm = pl.BlockSpec(memory_space=pltpu.HBM)


def layer_norm(values):
    center = values - jnp.mean(values, axis=-1, keepdims=True)
    spread = jnp.mean(center * center, axis=-1, keepdims=True)
    return center * lax.rsqrt(spread + EPS)


def dot(left, right):
    return jnp.dot(left, right, preferred_element_type=f32)


def split_pair(pairs):
    rows, _, width = pairs.shape
    flat = pairs.astype(f32).reshape(rows, 2 * width).astype(bf16)
    return flat[:, :width], flat[:, width:]


def head_lanes(shape):
    return lax.broadcasted_iota(i32, shape, len(shape) - 1) // HEAD_DIM


def attend_heads(queries, keys, values, bias, heads):
    rows, width = queries.shape
    lanes = head_lanes((rows, width))
    stacked = jnp.concatenate(
        [jnp.where(lanes == h, queries, jnp.zeros_like(queries)) for h in heads], axis=0
    )
    scores = lax.dot_general(
        stacked, keys, (((1,), (1,)), ((), ())), preferred_element_type=f32
    ).reshape(len(heads), rows, keys.shape[0])
    scores = scores * SCALE
    if bias is not None:
        scores = scores + bias[None]
    row_max = jnp.max(scores, axis=-1, keepdims=True)
    weights = jnp.exp(scores - row_max)
    row_sum = jnp.sum(weights, axis=-1, keepdims=True)
    summed = dot(weights.astype(bf16).reshape(len(heads) * rows, -1), values)
    summed = summed.reshape(len(heads), rows, width) / row_sum
    result = jnp.zeros((rows, width), f32)
    for i, h in enumerate(heads):
        result = jnp.where(lanes == h, summed[i], result)
    return result


def attend(queries, keys, values, bias):
    rows, width = queries.shape
    heads = list(range(width // HEAD_DIM))
    if len(heads) * rows * keys.shape[0] * 4 <= WIDE_SCORES:
        return attend_heads(queries, keys, values, bias, heads).astype(bf16)
    result = attend_heads(queries, keys, values, bias, heads[:1])
    for h in heads[1:]:
        result = result + attend_heads(queries, keys, values, bias, [h])
    return result.astype(bf16)


def request_info(token_ids, length_of, requests):
    request = jnp.zeros_like(token_ids)
    first_token = jnp.zeros_like(token_ids)
    end = jnp.int32(0)
    for i in range(requests):
        end = end + length_of(i)
        before = end <= token_ids
        request = request + before.astype(i32)
        first_token = jnp.where(before, first_token + length_of(i), first_token)
    return request, token_ids - first_token


def columns_body(pool, *outs):
    width = outs[0].shape[-1]
    for by, out in zip(rounds(len(outs)), outs):
        first = pl.multiple_of(partner(by) * width, width)
        out[...] = pool[0, :, :, :, pl.ds(first, width)]


def project_body(
    sizes, lengths_in, table_in, tokens, w_query, w_keyvalue, queries, keyvalue, bias, residual,
    lengths, table, sems,
):
    near, tok_count, head_count, shard_blocks, block_len = sizes
    requests = lengths.shape[1]
    copies = [
        pltpu.make_async_copy(lengths_in, lengths, sems.at[0]),
        pltpu.make_async_copy(table_in, table, sems.at[1]),
    ]
    for copy in copies:
        copy.start()
    normed = layer_norm(tokens[0].astype(f32)).astype(bf16)
    queries[...] = dot(normed, w_query[...]).astype(bf16)
    w_key, w_value = split_pair(w_keyvalue[...])
    rows, width = queries.shape
    keyvalue[:, :width] = dot(normed, w_key).astype(bf16)
    keyvalue[:, width:] = dot(normed, w_value).astype(bf16)

    for copy in copies:
        copy.wait()
    tok_index, head_index = lax.axis_index("tok"), lax.axis_index("head")
    share = residual.shape[0]
    start = pl.multiple_of(head_index * share, share)
    residual[...] = tokens[0, pl.ds(start, share), :].astype(f32)

    def length_of(i):
        return lengths[0, i]

    own_ids = tok_index * rows + lax.broadcasted_iota(i32, (rows, 1), 0)
    own_request, own_offset = request_info(own_ids, length_of, requests)
    for distance in range(near):
        ids = (tok_index - distance) * rows + lax.broadcasted_iota(i32, (1, rows), 1)
        allowed = (
            (ids >= 0)
            & (request_info(ids, length_of, requests)[0] == own_request)
            & (ids <= own_ids)
            & (own_ids - ids < WINDOW)
        )
        bias[:, distance * rows : (distance + 1) * rows] = jnp.where(allowed, 0.0, -jnp.inf)
    shard = head_count * shard_blocks * block_len
    prefix_len = tok_count * shard
    slot = lax.broadcasted_iota(i32, (1, shard), 1)
    for far in range(tok_count):
        places = slot % block_len
        for block in range(head_count * shard_blocks):
            owner = (tok_index ^ far) * head_count + partner(
                rounds(head_count)[block // shard_blocks]
            )
            logical = table[0, owner * shard_blocks + block % shard_blocks]
            places = places + jnp.where(slot // block_len == block, logical * block_len, 0)
        allowed = (places < SINK) | (places > prefix_len + own_offset - WINDOW)
        first = near * rows + far * shard
        bias[:, first : first + shard] = jnp.where(allowed, 0.0, -jnp.inf)


def self_body(near, head_count, queries, bias, w_out, *refs):
    term, refs = refs[-1], refs[:-1]
    near_refs, refs = refs[:near], refs[near:]
    slot_refs, outs = refs[:-head_count], refs[-head_count:]
    rows, width = queries.shape
    keys = [ref[:, :width] for ref in near_refs]
    values = [ref[:, width:] for ref in near_refs]
    for ref in slot_refs:
        key, value = split_pair(ref[...].reshape(ref.shape[0] * ref.shape[1], 2, width))
        keys.append(key)
        values.append(value)
    attended = attend(
        queries[...], jnp.concatenate(keys, axis=0), jnp.concatenate(values, axis=0), bias[...]
    )
    share = rows // head_count
    term[...] = dot(attended, w_out[...]).astype(bf16)
    for by, out in zip(rounds(head_count), outs):
        start = pl.multiple_of(partner(by) * share, share)
        out[...] = term[pl.ds(start, share), :]


def cross_body(w_cross_query, cross_cache, w_cross_out, *refs):
    rows_in, outs = refs[: len(refs) // 2], refs[len(refs) // 2 :]
    normed = jnp.concatenate([ref[...] for ref in rows_in], axis=0)
    queries = dot(normed, w_cross_query[...]).astype(bf16)
    keys, values = split_pair(cross_cache[0])
    cross_out = attend(queries, keys, values, None)
    term = dot(cross_out, w_cross_out[...]).astype(bf16)
    share = rows_in[0].shape[0]
    for i, out in enumerate(outs):
        out[...] = term[i * share : (i + 1) * share]


def after_body(head_count, before, *refs):
    terms, (after, *outs) = refs[:head_count], refs[head_count:]
    total = before[...] + sum(term[...].astype(f32) for term in terms)
    after[...] = total
    normed = layer_norm(total).astype(bf16)
    for out in outs:
        out[...] = normed


def hidden_body(w_up, w_down, *refs):
    rows_in, outs = refs[: len(refs) // 2], refs[len(refs) // 2 :]
    normed = jnp.concatenate([ref[...] for ref in rows_in], axis=0)
    if normed.shape[0] < FULL_ROWS:
        normed = jnp.concatenate([normed] * (FULL_ROWS // normed.shape[0]), axis=0)
    hidden = jax.nn.relu(dot(normed, w_up[...])).astype(bf16)
    term = dot(hidden, w_down[...]).astype(bf16)
    share = rows_in[0].shape[0]
    for i, out in enumerate(outs):
        out[...] = term[i * share : (i + 1) * share]


def on_device(
    tokens,
    lengths,
    block_position,
    prefix_pool,
    cross_cache,
    w_query,
    w_keyvalue,
    w_out,
    w_cross_query,
    w_cross_out,
    w_up,
    w_down,
):
    rows, model_width = tokens.shape[1:]
    width = w_query.shape[1]
    tok_count, head_count = lax.axis_size("tok"), lax.axis_size("head")
    share = rows // head_count
    shard_blocks, block_len = prefix_pool.shape[1:3]
    near_count = 1 + min(SPAN, tok_count - 1)
    key_count = near_count * rows + block_position.shape[1] * block_len
    sizes = (near_count, tok_count, head_count, shard_blocks, block_len)
    shape = jax.ShapeDtypeStruct
    row_pieces = [shape((share, model_width), bf16)] * head_count
    stats = [shape((share, model_width), f32)] + row_pieces

    pool_columns = kernel_call(
        columns_body,
        [shape((shard_blocks, block_len, 2, width), bf16)] * head_count,
        SMALL_VMEM,
        [],
        [],
        None,
        prefix_pool,
    )
    slots = exchange_heads(pool_columns)
    queries, keyvalue, bias, residual = kernel_call(
        functools.partial(project_body, sizes),
        [
            shape((rows, width), bf16),
            shape((rows, 2 * width), bf16),
            shape((rows, key_count), f32),
            shape((share, model_width), f32),
        ],
        2 * SMALL_VMEM,
        [
            pltpu.SMEM(lengths.shape, i32),
            pltpu.SMEM(block_position.shape, i32),
            pltpu.SemaphoreType.DMA((2,)),
        ],
        [in_hbm, in_hbm],
        None,
        lengths,
        block_position,
        tokens,
        w_query,
        w_keyvalue,
    )
    near = [keyvalue] + [
        from_behind(keyvalue, "tok", distance) for distance in range(1, near_count)
    ]
    all_slots = list(slots)
    for by in range(1, tok_count):
        for i, piece in enumerate(slots):
            ready = keyvalue if i < 3 else all_slots[-2]
            piece, _ = lax.optimization_barrier((piece, ready))
            all_slots.append(swap(piece, "tok", by))
    terms = kernel_call(
        functools.partial(self_body, near_count, head_count),
        row_pieces,
        SMALL_VMEM + 36 * rows * key_count,
        [pltpu.VMEM((rows, model_width), bf16)],
        [],
        None,
        queries,
        bias,
        w_out,
        *near,
        *all_slots,
    )
    after_self, *normed = kernel_call(
        functools.partial(after_body, head_count), stats, SMALL_VMEM, [], [], None, residual, *exchange_heads(terms)
    )
    arrived = exchange_heads(normed)
    terms = []
    for rows_in in (arrived[: head_count // 2], arrived[head_count // 2 :]):
        terms += kernel_call(
            cross_body,
            row_pieces[: len(rows_in)],
            SMALL_VMEM,
            [],
            [],
            None,
            w_cross_query,
            cross_cache,
            w_cross_out,
            *rows_in,
        )
    after_cross, *normed = kernel_call(
        functools.partial(after_body, head_count), stats, SMALL_VMEM, [], [], None, after_self, *exchange_heads(terms)
    )
    arrived = exchange_heads(normed)
    terms = []
    for rows_in in (arrived[: head_count // 2], arrived[head_count // 2 :]):
        terms += kernel_call(
            hidden_body,
            row_pieces[: len(rows_in)],
            2 * SMALL_VMEM,
            [],
            [],
            None,
            w_up,
            w_down,
            *rows_in,
        )
    result = after_cross + sum(term.astype(f32) for term in exchange_heads(terms))
    return result.astype(bf16)[None]


def solution(mesh):
    return jax.shard_map(
        on_device,
        mesh=mesh,
        in_specs=(
            P("grp", "tok", None),
            P("grp", None),
            P("grp", None),
            P("grp", ("tok", "head"), None, None, None),
            P("grp", None, None, "head"),
            P(None, "head"),
            P(None, None, "head"),
            P("head", None),
            P(None, "head"),
            P("head", None),
            P(None, "head"),
            P("head", None),
        ),
        out_specs=P("grp", ("tok", "head"), None),
        check_vma=False,
    )
```

```python
import functools

import jax
import jax.numpy as jnp
from jax import lax
from jax.experimental import pallas as pl
from jax.experimental.pallas import tpu as pltpu
from jax.sharding import PartitionSpec as P

HEAD_DIM = 64
SPAN = 8
SINK = 4
WINDOW = 1024
SCALE = HEAD_DIM ** (-0.5)
EPS = 1e-05
SMALL_VMEM = 12 << 20
KERNEL_FLOPS = 4 * 10**9
WIDE_SCORES = 8 << 20
FULL_ROWS = 128
LANES = 128

POOL_ORDER = (0, 3, 1, 2)
SELF_SUM_ORDER = (0, 2, 1, 3)
CROSS_ROWS_ORDER = (0, 3, 1, 2)
CROSS_SUM_ORDER = (0, 1, 3, 2)
HIDDEN_ROWS_ORDER = (0, 3, 2, 1)
HIDDEN_SUM_ORDER = (0, 3, 1, 2)

bf16 = jnp.bfloat16
f32 = jnp.float32
i32 = jnp.int32


def swap(array, axis, by):
    count = lax.axis_size(axis)
    return lax.ppermute(array, axis, [(i, i ^ by) for i in range(count)])


def from_behind(array, axis, by):
    count = lax.axis_size(axis)
    return lax.ppermute(array, axis, [(i, (i + by) % count) for i in range(count)])


def exchange_heads(pieces, order):
    return [swap(pieces[by], "head", by) if by else pieces[0] for by in order]


def partner(by):
    return lax.axis_index("head") ^ by


def kernel_call(body, outs, vmem_bytes, scratch, specs, out_specs, *args):
    return pl.pallas_call(
        body,
        out_shape=outs,
        in_specs=list(specs) + [pl.BlockSpec()] * (len(args) - len(specs)),
        out_specs=out_specs or [pl.BlockSpec()] * len(outs),
        scratch_shapes=scratch,
        compiler_params=pltpu.CompilerParams(vmem_limit_bytes=vmem_bytes),
        cost_estimate=pl.CostEstimate(
            flops=KERNEL_FLOPS, bytes_accessed=sum(a.nbytes for a in args), transcendentals=0
        ),
    )(*args)


in_hbm = pl.BlockSpec(memory_space=pltpu.HBM)


def layer_norm(values):
    center = values - jnp.mean(values, axis=-1, keepdims=True)
    spread = jnp.mean(center * center, axis=-1, keepdims=True)
    return center * lax.rsqrt(spread + EPS)


def dot(left, right):
    return jnp.dot(left, right, preferred_element_type=f32)


def split_pair(pairs):
    rows, _, width = pairs.shape
    flat = pairs.astype(f32).reshape(rows, 2 * width).astype(bf16)
    return flat[:, :width], flat[:, width:]


def head_lanes(shape):
    return lax.broadcasted_iota(i32, shape, len(shape) - 1) // HEAD_DIM


def head_sets(rows, width, keys):
    heads = list(range(width // HEAD_DIM))
    if len(heads) * rows * keys * 4 <= WIDE_SCORES:
        return [heads]
    return [[h] for h in heads]


def head_scores(queries, keys, bias, heads):
    lanes = head_lanes(queries.shape)
    stacked = jnp.concatenate(
        [jnp.where(lanes == h, queries, jnp.zeros_like(queries)) for h in heads], axis=0
    )
    scores = lax.dot_general(
        stacked, keys, (((1,), (1,)), ((), ())), preferred_element_type=f32
    ).reshape(len(heads), queries.shape[0], keys.shape[0])
    scores = scores * SCALE
    return scores if bias is None else scores + bias[None]


def weigh(weights, values):
    heads, rows, keys = weights.shape
    return dot(weights.astype(bf16).reshape(heads * rows, keys), values).reshape(heads, rows, -1)


def own_lanes(per_head, heads):
    lanes = head_lanes(per_head.shape[1:])
    result = jnp.zeros(per_head.shape[1:], f32)
    for i, h in enumerate(heads):
        result = jnp.where(lanes == h, per_head[i], result)
    return result


def attend(queries, keys, values):
    result = 0.0
    for heads in head_sets(*queries.shape, keys.shape[0]):
        scores = head_scores(queries, keys, None, heads)
        weights = jnp.exp(scores - jnp.max(scores, axis=-1, keepdims=True))
        row_sum = jnp.sum(weights, axis=-1, keepdims=True)
        result = result + own_lanes(weigh(weights, values) / row_sum, heads)
    return result.astype(bf16)


def request_info(token_ids, length_of, requests):
    request = jnp.zeros_like(token_ids)
    first_token = jnp.zeros_like(token_ids)
    end = jnp.int32(0)
    for i in range(requests):
        end = end + length_of(i)
        before = end <= token_ids
        request = request + before.astype(i32)
        first_token = jnp.where(before, first_token + length_of(i), first_token)
    return request, token_ids - first_token


def columns_body(pool, *outs):
    width = outs[0].shape[-1]
    for by, out in enumerate(outs):
        first = pl.multiple_of(partner(by) * width, width)
        out[...] = pool[0, :, :, :, pl.ds(first, width)]


def project_body(
    sizes, lengths_in, table_in, tokens, w_query, w_keyvalue, queries, keyvalue, bias, far_bias, residual,
    lengths, table, sems,
):
    near, tok_count, head_count, shard_blocks, block_len = sizes
    requests = lengths.shape[1]
    copies = [
        pltpu.make_async_copy(lengths_in, lengths, sems.at[0]),
        pltpu.make_async_copy(table_in, table, sems.at[1]),
    ]
    for copy in copies:
        copy.start()
    normed = layer_norm(tokens[0].astype(f32)).astype(bf16)
    queries[...] = dot(normed, w_query[...]).astype(bf16)
    w_key, w_value = split_pair(w_keyvalue[...])
    rows, width = queries.shape
    keyvalue[:, :width] = dot(normed, w_key).astype(bf16)
    keyvalue[:, width:] = dot(normed, w_value).astype(bf16)

    for copy in copies:
        copy.wait()
    tok_index, head_index = lax.axis_index("tok"), lax.axis_index("head")
    share = residual.shape[0]
    start = pl.multiple_of(head_index * share, share)
    residual[...] = tokens[0, pl.ds(start, share), :].astype(f32)

    def length_of(i):
        return lengths[0, i]

    own_ids = tok_index * rows + lax.broadcasted_iota(i32, (rows, 1), 0)
    own_request, own_offset = request_info(own_ids, length_of, requests)
    for distance in range(near):
        ids = (tok_index - distance) * rows + lax.broadcasted_iota(i32, (1, rows), 1)
        allowed = (
            (ids >= 0)
            & (request_info(ids, length_of, requests)[0] == own_request)
            & (ids <= own_ids)
            & (own_ids - ids < WINDOW)
        )
        out, first = (far_bias, (distance - 1) * rows) if distance else (bias, 0)
        out[:, first : first + rows] = jnp.where(allowed, 0.0, -jnp.inf)
    shard = head_count * shard_blocks * block_len
    prefix_len = tok_count * shard
    slot = lax.broadcasted_iota(i32, (1, shard), 1)
    for far in range(tok_count):
        places = slot % block_len
        for block in range(head_count * shard_blocks):
            owner = (tok_index ^ far) * head_count + partner(
                POOL_ORDER[block // shard_blocks]
            )
            logical = table[0, owner * shard_blocks + block % shard_blocks]
            places = places + jnp.where(slot // block_len == block, logical * block_len, 0)
        allowed = (places < SINK) | (places > prefix_len + own_offset - WINDOW)
        out, first = (far_bias, (near - 1) * rows + (far - 1) * shard) if far else (bias, rows)
        out[:, first : first + shard] = jnp.where(allowed, 0.0, -jnp.inf)


def gather_keys(suffix_refs, slot_refs, width):
    pairs = [split_pair(r[...].reshape(r.shape[0] * r.shape[1], 2, width)) for r in slot_refs]
    keys = [ref[:, :width] for ref in suffix_refs] + [key for key, _ in pairs]
    values = [ref[:, width:] for ref in suffix_refs] + [value for _, value in pairs]
    return jnp.concatenate(keys, axis=0), jnp.concatenate(values, axis=0)


def near_body(queries, bias, keyvalue, *refs):
    *slot_refs, maxima, sums, weighted = refs
    rows, width = queries.shape
    keys, values = gather_keys([keyvalue], slot_refs, width)
    for heads in head_sets(rows, width, keys.shape[0]):
        scores = head_scores(queries[...], keys, bias[...], heads)
        row_max = jnp.max(scores, axis=-1, keepdims=True)
        weights = jnp.exp(scores - row_max)
        row_sum = jnp.sum(weights, axis=-1, keepdims=True)
        chosen = slice(heads[0], heads[-1] + 1)
        shape = (len(heads), rows, LANES)
        maxima[chosen] = jnp.broadcast_to(row_max, shape)
        sums[chosen] = jnp.broadcast_to(row_sum, shape)
        weighted[chosen] = weigh(weights, values)


def far_body(behind, head_count, queries, bias, w_out, maxima, sums, weighted, *refs):
    *refs, term = refs
    slot_refs, outs = refs[:-head_count], refs[-head_count:]
    rows, width = queries.shape
    keys, values = gather_keys(slot_refs[:behind], slot_refs[behind:], width)

    def spread(array, size):
        return jnp.concatenate([array] * (size // LANES), axis=-1)

    attended = 0.0
    for heads in head_sets(rows, width, keys.shape[0]):
        chosen = slice(heads[0], heads[-1] + 1)
        scores = head_scores(queries[...], keys, bias[...], heads)
        before = maxima[chosen]
        row_max = jnp.maximum(before, jnp.max(scores, axis=-1, keepdims=True))
        weights = jnp.exp(scores - spread(row_max, keys.shape[0]))
        scale = jnp.exp(before - row_max)
        row_sum = jnp.sum(weights, axis=-1, keepdims=True) + scale * sums[chosen]
        total = weigh(weights, values) + spread(scale, width) * weighted[chosen]
        here = own_lanes(jnp.ones_like(total), heads)
        total, row_sum = own_lanes(total, heads), own_lanes(spread(row_sum, width), heads)
        attended = attended + total / jnp.where(here > 0, row_sum, 1.0)
    share = rows // head_count
    term[...] = dot(attended.astype(bf16), w_out[...]).astype(bf16)
    for by, out in enumerate(outs):
        start = pl.multiple_of(partner(by) * share, share)
        out[...] = term[pl.ds(start, share), :]


def cross_body(w_cross_query, cross_cache, w_cross_out, *refs):
    rows_in, outs = refs[: len(refs) // 2], refs[len(refs) // 2 :]
    normed = jnp.concatenate([ref[...] for ref in rows_in], axis=0)
    queries = dot(normed, w_cross_query[...]).astype(bf16)
    keys, values = split_pair(cross_cache[0])
    cross_out = attend(queries, keys, values)
    term = dot(cross_out, w_cross_out[...]).astype(bf16)
    share = rows_in[0].shape[0]
    for i, out in enumerate(outs):
        out[...] = term[i * share : (i + 1) * share]


def after_body(head_count, before, *refs):
    terms, (after, *outs) = refs[:head_count], refs[head_count:]
    total = before[...] + sum(term[...].astype(f32) for term in terms)
    after[...] = total
    normed = layer_norm(total).astype(bf16)
    for out in outs:
        out[...] = normed


def result_body(before, *refs):
    *terms, out = refs
    out[0] = (before[...] + sum(term[...].astype(f32) for term in terms)).astype(bf16)


def hidden_body(w_up, w_down, *refs):
    rows_in, outs = refs[: len(refs) // 2], refs[len(refs) // 2 :]
    normed = jnp.concatenate([ref[...] for ref in rows_in], axis=0)
    if normed.shape[0] < FULL_ROWS:
        normed = jnp.concatenate([normed] * (FULL_ROWS // normed.shape[0]), axis=0)
    hidden = jax.nn.relu(dot(normed, w_up[...])).astype(bf16)
    term = dot(hidden, w_down[...]).astype(bf16)
    share = rows_in[0].shape[0]
    for i, out in enumerate(outs):
        out[...] = term[i * share : (i + 1) * share]


def on_device(
    tokens,
    lengths,
    block_position,
    prefix_pool,
    cross_cache,
    w_query,
    w_keyvalue,
    w_out,
    w_cross_query,
    w_cross_out,
    w_up,
    w_down,
):
    rows, model_width = tokens.shape[1:]
    width = w_query.shape[1]
    tok_count, head_count = lax.axis_size("tok"), lax.axis_size("head")
    share = rows // head_count
    shard_blocks, block_len = prefix_pool.shape[1:3]
    near_count = 1 + min(SPAN, tok_count - 1)
    slot_count = head_count * shard_blocks * block_len
    sizes = (near_count, tok_count, head_count, shard_blocks, block_len)
    shape = jax.ShapeDtypeStruct
    row_pieces = [shape((share, model_width), bf16)] * head_count
    stats = [shape((share, model_width), f32)] + row_pieces

    pool_columns = kernel_call(
        columns_body,
        [shape((shard_blocks, block_len, 2, width), bf16)] * head_count,
        SMALL_VMEM,
        [],
        [],
        None,
        prefix_pool,
    )
    slots = exchange_heads(pool_columns, POOL_ORDER)
    queries, keyvalue, bias, far_bias, residual = kernel_call(
        functools.partial(project_body, sizes),
        [
            shape((rows, width), bf16),
            shape((rows, 2 * width), bf16),
            shape((rows, rows + slot_count), f32),
            shape((rows, (near_count - 1) * rows + (tok_count - 1) * slot_count), f32),
            shape((share, model_width), f32),
        ],
        2 * SMALL_VMEM,
        [
            pltpu.SMEM(lengths.shape, i32),
            pltpu.SMEM(block_position.shape, i32),
            pltpu.SemaphoreType.DMA((2,)),
        ],
        [in_hbm, in_hbm],
        None,
        lengths,
        block_position,
        tokens,
        w_query,
        w_keyvalue,
    )
    behind = [from_behind(keyvalue, "tok", distance) for distance in range(1, near_count)]
    far_slots = []
    for by in range(1, tok_count):
        for i, piece in enumerate(slots):
            ready = far_slots[-2] if i == len(slots) - 1 else keyvalue
            piece, _ = lax.optimization_barrier((piece, ready))
            far_slots.append(swap(piece, "tok", by))
    heads = width // HEAD_DIM
    partial = kernel_call(
        near_body,
        [shape((heads, rows, LANES), f32)] * 2 + [shape((heads, rows, width), f32)],
        SMALL_VMEM + 36 * bias.size,
        [],
        [],
        None,
        queries,
        bias,
        keyvalue,
        *slots,
    )
    terms = kernel_call(
        functools.partial(far_body, len(behind), head_count),
        row_pieces,
        SMALL_VMEM + 36 * far_bias.size,
        [pltpu.VMEM((rows, model_width), bf16)],
        [],
        None,
        queries,
        far_bias,
        w_out,
        *partial,
        *behind,
        *far_slots,
    )
    after_self, *normed = kernel_call(
        functools.partial(after_body, head_count), stats, SMALL_VMEM, [], [], None, residual, *exchange_heads(terms, SELF_SUM_ORDER)
    )
    arrived = exchange_heads(normed, CROSS_ROWS_ORDER)
    terms = []
    for rows_in in (arrived[: head_count // 2], arrived[head_count // 2 :]):
        *rows_in, _ = lax.optimization_barrier((*rows_in, terms))
        terms += kernel_call(
            cross_body,
            row_pieces[: len(rows_in)],
            SMALL_VMEM,
            [],
            [],
            None,
            w_cross_query,
            cross_cache,
            w_cross_out,
            *rows_in,
        )
    terms = [terms[CROSS_ROWS_ORDER.index(by)] for by in range(head_count)]
    after_cross, *normed = kernel_call(
        functools.partial(after_body, head_count), stats, SMALL_VMEM, [], [], None, after_self, *exchange_heads(terms, CROSS_SUM_ORDER)
    )
    arrived = exchange_heads(normed, HIDDEN_ROWS_ORDER)
    terms = []
    for rows_in in (arrived[: head_count // 2], arrived[head_count // 2 :]):
        *rows_in, _ = lax.optimization_barrier((*rows_in, terms))
        terms += kernel_call(
            hidden_body,
            row_pieces[: len(rows_in)],
            2 * SMALL_VMEM,
            [],
            [],
            None,
            w_up,
            w_down,
            *rows_in,
        )
    terms = [terms[HIDDEN_ROWS_ORDER.index(by)] for by in range(head_count)]
    return kernel_call(
        result_body,
        [shape((1, share, model_width), bf16)],
        SMALL_VMEM,
        [],
        [],
        None,
        after_cross,
        *exchange_heads(terms, HIDDEN_SUM_ORDER),
    )[0]


def solution(mesh):
    return jax.shard_map(
        on_device,
        mesh=mesh,
        in_specs=(
            P("grp", "tok", None),
            P("grp", None),
            P("grp", None),
            P("grp", ("tok", "head"), None, None, None),
            P("grp", None, None, "head"),
            P(None, "head"),
            P(None, None, "head"),
            P("head", None),
            P(None, "head"),
            P("head", None),
            P(None, "head"),
            P("head", None),
        ),
        out_specs=P("grp", ("tok", "head"), None),
        check_vma=False,
    )
```

```python
import functools

import jax
import jax.numpy as jnp
from jax import lax
from jax.experimental import pallas as pl
from jax.experimental.pallas import tpu as pltpu
from jax.sharding import PartitionSpec as P

HEAD_DIM = 64
SPAN = 8
SINK = 4
WINDOW = 1024
SCALE = HEAD_DIM ** (-0.5)
EPS = 1e-05
SMALL_VMEM = 12 << 20
KERNEL_FLOPS = 4 * 10**9
WIDE_SCORES = 8 << 20
FULL_ROWS = 128
LANES = 128

POOL_ORDER = (0, 3, 1, 2)
SELF_SUM_ORDER = (0, 2, 1, 3)
CROSS_ROWS_ORDER = (0, 3, 1, 2)
CROSS_SUM_ORDER = (0, 1, 3, 2)
HIDDEN_ROWS_ORDER = (0, 3, 2, 1)
HIDDEN_SUM_ORDER = (0, 3, 1, 2)

bf16 = jnp.bfloat16
f32 = jnp.float32
i32 = jnp.int32


def swap(array, axis, by):
    count = lax.axis_size(axis)
    return lax.ppermute(array, axis, [(i, i ^ by) for i in range(count)])


def from_behind(array, axis, by):
    count = lax.axis_size(axis)
    return lax.ppermute(array, axis, [(i, (i + by) % count) for i in range(count)])


def exchange_heads(pieces, order):
    return [swap(pieces[by], "head", by) if by else pieces[0] for by in order]


def partner(by):
    return lax.axis_index("head") ^ by


def kernel_call(body, outs, vmem_bytes, scratch, specs, out_specs, *args):
    return pl.pallas_call(
        body,
        out_shape=outs,
        in_specs=list(specs) + [pl.BlockSpec()] * (len(args) - len(specs)),
        out_specs=out_specs or [pl.BlockSpec()] * len(outs),
        scratch_shapes=scratch,
        compiler_params=pltpu.CompilerParams(vmem_limit_bytes=vmem_bytes),
        cost_estimate=pl.CostEstimate(
            flops=KERNEL_FLOPS, bytes_accessed=sum(a.nbytes for a in args), transcendentals=0
        ),
    )(*args)


in_hbm = pl.BlockSpec(memory_space=pltpu.HBM)


def layer_norm(values):
    center = values - jnp.mean(values, axis=-1, keepdims=True)
    spread = jnp.mean(center * center, axis=-1, keepdims=True)
    return center * lax.rsqrt(spread + EPS)


def dot(left, right):
    return jnp.dot(left, right, preferred_element_type=f32)


def split_pair(pairs):
    rows, _, width = pairs.shape
    flat = pairs.astype(f32).reshape(rows, 2 * width).astype(bf16)
    return flat[:, :width], flat[:, width:]


def head_lanes(shape):
    return lax.broadcasted_iota(i32, shape, len(shape) - 1) // HEAD_DIM


def head_sets(rows, width, keys):
    heads = list(range(width // HEAD_DIM))
    if len(heads) * rows * keys * 4 <= WIDE_SCORES:
        return [heads]
    return [[h] for h in heads]


def head_scores(queries, keys, bias, heads):
    lanes = head_lanes(queries.shape)
    stacked = jnp.concatenate(
        [jnp.where(lanes == h, queries, jnp.zeros_like(queries)) for h in heads], axis=0
    )
    scores = lax.dot_general(
        stacked, keys, (((1,), (1,)), ((), ())), preferred_element_type=f32
    ).reshape(len(heads), queries.shape[0], keys.shape[0])
    scores = scores * SCALE
    return scores if bias is None else scores + bias[None]


def weigh(weights, values):
    heads, rows, keys = weights.shape
    return dot(weights.astype(bf16).reshape(heads * rows, keys), values).reshape(heads, rows, -1)


def own_lanes(per_head, heads):
    lanes = head_lanes(per_head.shape[1:])
    result = jnp.zeros(per_head.shape[1:], f32)
    for i, h in enumerate(heads):
        result = jnp.where(lanes == h, per_head[i], result)
    return result


def attend(queries, keys, values):
    result = 0.0
    for heads in head_sets(*queries.shape, keys.shape[0]):
        scores = head_scores(queries, keys, None, heads)
        weights = jnp.exp(scores - jnp.max(scores, axis=-1, keepdims=True))
        row_sum = jnp.sum(weights, axis=-1, keepdims=True)
        result = result + own_lanes(weigh(weights, values) / row_sum, heads)
    return result.astype(bf16)


def request_info(token_ids, length_of, requests):
    request = jnp.zeros_like(token_ids)
    first_token = jnp.zeros_like(token_ids)
    end = jnp.int32(0)
    for i in range(requests):
        end = end + length_of(i)
        before = end <= token_ids
        request = request + before.astype(i32)
        first_token = jnp.where(before, first_token + length_of(i), first_token)
    return request, token_ids - first_token


def columns_body(pool, *outs):
    width = outs[0].shape[-1]
    for by, out in enumerate(outs):
        first = pl.multiple_of(partner(by) * width, width)
        out[...] = pool[0, :, :, :, pl.ds(first, width)]


def project_body(
    sizes, lengths_in, table_in, tokens, w_query, w_keyvalue, queries, keyvalue, bias, far_bias, residual,
    lengths, table, sems,
):
    near, tok_count, head_count, shard_blocks, block_len = sizes
    requests = lengths.shape[1]
    copies = [
        pltpu.make_async_copy(lengths_in, lengths, sems.at[0]),
        pltpu.make_async_copy(table_in, table, sems.at[1]),
    ]
    for copy in copies:
        copy.start()
    normed = layer_norm(tokens[0].astype(f32)).astype(bf16)
    queries[...] = dot(normed, w_query[...]).astype(bf16)
    w_key, w_value = split_pair(w_keyvalue[...])
    rows, width = queries.shape
    keyvalue[:, :width] = dot(normed, w_key).astype(bf16)
    keyvalue[:, width:] = dot(normed, w_value).astype(bf16)

    for copy in copies:
        copy.wait()
    tok_index, head_index = lax.axis_index("tok"), lax.axis_index("head")
    share = residual.shape[0]
    start = pl.multiple_of(head_index * share, share)
    residual[...] = tokens[0, pl.ds(start, share), :].astype(f32)

    def length_of(i):
        return lengths[0, i]

    own_ids = tok_index * rows + lax.broadcasted_iota(i32, (rows, 1), 0)
    own_request, own_offset = request_info(own_ids, length_of, requests)
    for distance in range(near):
        ids = (tok_index - distance) * rows + lax.broadcasted_iota(i32, (1, rows), 1)
        allowed = (
            (ids >= 0)
            & (request_info(ids, length_of, requests)[0] == own_request)
            & (ids <= own_ids)
            & (own_ids - ids < WINDOW)
        )
        out, first = (far_bias, (distance - 1) * rows) if distance else (bias, 0)
        out[:, first : first + rows] = jnp.where(allowed, 0.0, -jnp.inf)
    shard = head_count * shard_blocks * block_len
    prefix_len = tok_count * shard
    slot = lax.broadcasted_iota(i32, (1, shard), 1)
    for far in range(tok_count):
        places = slot % block_len
        for block in range(head_count * shard_blocks):
            owner = (tok_index ^ far) * head_count + partner(
                POOL_ORDER[block // shard_blocks]
            )
            logical = table[0, owner * shard_blocks + block % shard_blocks]
            places = places + jnp.where(slot // block_len == block, logical * block_len, 0)
        allowed = (places < SINK) | (places > prefix_len + own_offset - WINDOW)
        out, first = (far_bias, (near - 1) * rows + (far - 1) * shard) if far else (bias, rows)
        out[:, first : first + shard] = jnp.where(allowed, 0.0, -jnp.inf)


def gather_keys(suffix_refs, slot_refs, width):
    pairs = [split_pair(r[...].reshape(r.shape[0] * r.shape[1], 2, width)) for r in slot_refs]
    keys = [ref[:, :width] for ref in suffix_refs] + [key for key, _ in pairs]
    values = [ref[:, width:] for ref in suffix_refs] + [value for _, value in pairs]
    return jnp.concatenate(keys, axis=0), jnp.concatenate(values, axis=0)


def near_body(queries, bias, keyvalue, *refs):
    *slot_refs, maxima, sums, weighted = refs
    rows, width = queries.shape
    keys, values = gather_keys([keyvalue], slot_refs, width)
    for heads in head_sets(rows, width, keys.shape[0]):
        scores = head_scores(queries[...], keys, bias[...], heads)
        row_max = jnp.max(scores, axis=-1, keepdims=True)
        weights = jnp.exp(scores - row_max)
        row_sum = jnp.sum(weights, axis=-1, keepdims=True)
        chosen = slice(heads[0], heads[-1] + 1)
        shape = (len(heads), rows, LANES)
        maxima[chosen] = jnp.broadcast_to(row_max, shape)
        sums[chosen] = jnp.broadcast_to(row_sum, shape)
        weighted[chosen] = weigh(weights, values)


def far_body(behind, head_count, queries, bias, w_out, maxima, sums, weighted, *refs):
    *refs, term = refs
    slot_refs, outs = refs[:-head_count], refs[-head_count:]
    rows, width = queries.shape
    keys, values = gather_keys(slot_refs[:behind], slot_refs[behind:], width)

    def spread(array, size):
        return jnp.concatenate([array] * (size // LANES), axis=-1)

    attended = 0.0
    for heads in head_sets(rows, width, keys.shape[0]):
        chosen = slice(heads[0], heads[-1] + 1)
        scores = head_scores(queries[...], keys, bias[...], heads)
        before = maxima[chosen]
        row_max = jnp.maximum(before, jnp.max(scores, axis=-1, keepdims=True))
        weights = jnp.exp(scores - spread(row_max, keys.shape[0]))
        scale = jnp.exp(before - row_max)
        row_sum = jnp.sum(weights, axis=-1, keepdims=True) + scale * sums[chosen]
        total = weigh(weights, values) + spread(scale, width) * weighted[chosen]
        here = own_lanes(jnp.ones_like(total), heads)
        total, row_sum = own_lanes(total, heads), own_lanes(spread(row_sum, width), heads)
        attended = attended + total / jnp.where(here > 0, row_sum, 1.0)
    share = rows // head_count
    term[...] = dot(attended.astype(bf16), w_out[...]).astype(bf16)
    for by, out in enumerate(outs):
        start = pl.multiple_of(partner(by) * share, share)
        out[...] = term[pl.ds(start, share), :]


def cross_body(w_cross_query, cross_cache, w_cross_out, *refs):
    rows_in, outs = refs[: len(refs) // 2], refs[len(refs) // 2 :]
    normed = jnp.concatenate([ref[...] for ref in rows_in], axis=0)
    queries = dot(normed, w_cross_query[...]).astype(bf16)
    keys, values = split_pair(cross_cache[0])
    cross_out = attend(queries, keys, values)
    term = dot(cross_out, w_cross_out[...]).astype(bf16)
    share = rows_in[0].shape[0]
    for i, out in enumerate(outs):
        out[...] = term[i * share : (i + 1) * share]


def after_body(head_count, before, *refs):
    terms, (after, *outs) = refs[:head_count], refs[head_count:]
    total = before[...] + sum(term[...].astype(f32) for term in terms)
    after[...] = total
    normed = layer_norm(total).astype(bf16)
    for out in outs:
        out[...] = normed


def result_body(before, *refs):
    *terms, out = refs
    out[0] = (before[...] + sum(term[...].astype(f32) for term in terms)).astype(bf16)


def hidden_body(w_up, w_down, *refs):
    rows_in, outs = refs[: len(refs) // 2], refs[len(refs) // 2 :]
    normed = jnp.concatenate([ref[...] for ref in rows_in], axis=0)
    if normed.shape[0] < FULL_ROWS:
        normed = jnp.concatenate([normed] * (FULL_ROWS // normed.shape[0]), axis=0)
    hidden = jax.nn.relu(dot(normed, w_up[...])).astype(bf16)
    term = dot(hidden, w_down[...]).astype(bf16)
    share = rows_in[0].shape[0]
    for i, out in enumerate(outs):
        out[...] = term[i * share : (i + 1) * share]


def on_device(
    tokens,
    lengths,
    block_position,
    prefix_pool,
    cross_cache,
    w_query,
    w_keyvalue,
    w_out,
    w_cross_query,
    w_cross_out,
    w_up,
    w_down,
):
    rows, model_width = tokens.shape[1:]
    width = w_query.shape[1]
    tok_count, head_count = lax.axis_size("tok"), lax.axis_size("head")
    share = rows // head_count
    shard_blocks, block_len = prefix_pool.shape[1:3]
    near_count = 1 + min(SPAN, tok_count - 1)
    slot_count = head_count * shard_blocks * block_len
    sizes = (near_count, tok_count, head_count, shard_blocks, block_len)
    shape = jax.ShapeDtypeStruct
    row_pieces = [shape((share, model_width), bf16)] * head_count
    stats = [shape((share, model_width), f32)] + row_pieces

    pool_columns = kernel_call(
        columns_body,
        [shape((shard_blocks, block_len, 2, width), bf16)] * head_count,
        SMALL_VMEM,
        [],
        [],
        None,
        prefix_pool,
    )
    slots = exchange_heads(pool_columns, POOL_ORDER)
    w_keyvalue, w_query, _ = lax.optimization_barrier((w_keyvalue, w_query, pool_columns[0]))
    queries, keyvalue, bias, far_bias, residual = kernel_call(
        functools.partial(project_body, sizes),
        [
            shape((rows, width), bf16),
            shape((rows, 2 * width), bf16),
            shape((rows, rows + slot_count), f32),
            shape((rows, (near_count - 1) * rows + (tok_count - 1) * slot_count), f32),
            shape((share, model_width), f32),
        ],
        2 * SMALL_VMEM,
        [
            pltpu.SMEM(lengths.shape, i32),
            pltpu.SMEM(block_position.shape, i32),
            pltpu.SemaphoreType.DMA((2,)),
        ],
        [in_hbm, in_hbm],
        None,
        lengths,
        block_position,
        tokens,
        w_query,
        w_keyvalue,
    )
    behind = [from_behind(keyvalue, "tok", distance) for distance in range(1, near_count)]
    far_slots = []
    for by in range(1, tok_count):
        for i, piece in enumerate(slots):
            ready = far_slots[-2] if i == len(slots) - 1 else keyvalue
            piece, _ = lax.optimization_barrier((piece, ready))
            far_slots.append(swap(piece, "tok", by))
    heads = width // HEAD_DIM
    partial = kernel_call(
        near_body,
        [shape((heads, rows, LANES), f32)] * 2 + [shape((heads, rows, width), f32)],
        SMALL_VMEM + 36 * bias.size,
        [],
        [],
        None,
        queries,
        bias,
        keyvalue,
        *slots,
    )
    terms = kernel_call(
        functools.partial(far_body, len(behind), head_count),
        row_pieces,
        SMALL_VMEM + 36 * far_bias.size,
        [pltpu.VMEM((rows, model_width), bf16)],
        [],
        None,
        queries,
        far_bias,
        w_out,
        *partial,
        *behind,
        *far_slots,
    )
    after_self, *normed = kernel_call(
        functools.partial(after_body, head_count), stats, SMALL_VMEM, [], [], None, residual, *exchange_heads(terms, SELF_SUM_ORDER)
    )
    arrived = exchange_heads(normed, CROSS_ROWS_ORDER)
    terms = []
    for rows_in in (arrived[: head_count // 2], arrived[head_count // 2 :]):
        *rows_in, _ = lax.optimization_barrier((*rows_in, terms))
        terms += kernel_call(
            cross_body,
            row_pieces[: len(rows_in)],
            SMALL_VMEM,
            [],
            [],
            None,
            w_cross_query,
            cross_cache,
            w_cross_out,
            *rows_in,
        )
    terms = [terms[CROSS_ROWS_ORDER.index(by)] for by in range(head_count)]
    after_cross, *normed = kernel_call(
        functools.partial(after_body, head_count), stats, SMALL_VMEM, [], [], None, after_self, *exchange_heads(terms, CROSS_SUM_ORDER)
    )
    arrived = exchange_heads(normed, HIDDEN_ROWS_ORDER)
    terms = []
    for rows_in in (arrived[: head_count // 2], arrived[head_count // 2 :]):
        *rows_in, _ = lax.optimization_barrier((*rows_in, terms))
        terms += kernel_call(
            hidden_body,
            row_pieces[: len(rows_in)],
            2 * SMALL_VMEM,
            [],
            [],
            None,
            w_up,
            w_down,
            *rows_in,
        )
    terms = [terms[HIDDEN_ROWS_ORDER.index(by)] for by in range(head_count)]
    return kernel_call(
        result_body,
        [shape((1, share, model_width), bf16)],
        SMALL_VMEM,
        [],
        [],
        None,
        after_cross,
        *exchange_heads(terms, HIDDEN_SUM_ORDER),
    )[0]


def solution(mesh):
    return jax.shard_map(
        on_device,
        mesh=mesh,
        in_specs=(
            P("grp", "tok", None),
            P("grp", None),
            P("grp", None),
            P("grp", ("tok", "head"), None, None, None),
            P("grp", None, None, "head"),
            P(None, "head"),
            P(None, None, "head"),
            P("head", None),
            P(None, "head"),
            P("head", None),
            P(None, "head"),
            P("head", None),
        ),
        out_specs=P("grp", ("tok", "head"), None),
        check_vma=False,
    )
```
